32 devices in a mesh: tm: 8 (over z, y), space: 4 (over x, core).
Axes of the slice: x: 2, y: 2, z: 4, core: 2. Of those that a mesh axis runs over, the one named last changes fastest.
Arguments:
- frames: bfloat16 [128, 16, 64, 384], P('tm', 'space'), may hold values from -6 to 6
- token_ids: int32 [1, 128, 16, 64], P(None, 'tm', 'space'), may hold values from 0 to 1023
- action_ids: int32 [128], P('tm'), may hold values from 0 to 7
- token_table: bfloat16 [1024, 384], replicated, may hold values from -6 to 6
- action_table: bfloat16 [8, 384], replicated, may hold values from -3 to 3
- conv_weight: bfloat16 [3, 3, 384], replicated, may hold values from -1.796875 to 1.796875
- norm_gain: bfloat16 [384], replicated, may hold values from 0.5 to 1.5
- w_query: bfloat16 [384, 384], replicated, may hold values from -12 to 12
- w_key: bfloat16 [384, 384], replicated, may hold values from -12 to 12
- w_value: bfloat16 [384, 384], replicated, may hold values from -0.3125 to 0.3125
- w_out: bfloat16 [384, 384], replicated, may hold values from -0.625 to 0.625
Outputs:
- final_frames: bfloat16 [128, 16, 64, 384], P('tm', 'space')
The draws below stay inside these ranges and needn't reach their ends.
All inputs are finite; a program needn't handle non-finite values.
Results may differ from the reference program's by a relative error of at most 0.0057.
Values may be sent and summed in bfloat16 or wider, within the bound.
A program may use at most 192 MiB of HBM per device.

```python
import jax
import jax.numpy as jnp
from jax import lax

D = 384
HEADS = 6
VOCAB = 1024
ACTIONS = 8
GRID_ROWS = 16
GRID_COLS = 64
WINDOW = 16
ANCHORS = 4
STEPS = 1
FR_DEV = 16
FRAMES = 128


def draw_w_query(key, part):
    random_part = jax.random.normal(jax.random.fold_in(key, 1), (D, D), jnp.float32) / jnp.sqrt(jnp.float32(D))
    return random_part.astype(jnp.bfloat16)


def draw_w_key(key, part):
    random_part = jax.random.normal(jax.random.fold_in(key, 2), (D, D), jnp.float32) / jnp.sqrt(jnp.float32(D))
    return random_part.astype(jnp.bfloat16)


def set_ends(drawn, key, least, top_value):
    shape = drawn.shape
    index_at = [jax.random.randint(jax.random.fold_in(key, axis), (), 0, shape[axis]) for axis in range(len(shape))]
    drawn = drawn.at[tuple(index_at)].set(least)
    longest = shape.index(max(shape))
    index_at[longest] = (index_at[longest] + 1) % shape[longest]
    return drawn.at[tuple(index_at)].set(top_value)


def level_of(own_key, dims, pieces, least, top_value):
    gain = 1.0
    for axis_at, parts in pieces:
        heights = jax.random.uniform(jax.random.fold_in(jax.random.fold_in(own_key, 6), axis_at), (parts,), jnp.float32, least / len(pieces), top_value / len(pieces))
        gain = gain * jnp.repeat(jnp.exp(heights), dims[axis_at] // parts).reshape((-1,) + (1,) * (len(dims) - 1 - axis_at))
    return gain


def noise(key, extent, deviation, reach, shards=(), held_as=jnp.bfloat16):
    drawn = deviation * jax.random.normal(key, extent, jnp.float32)
    if shards:
        drawn = drawn * level_of(key, extent, shards, -0.22, 0.18)
    return jnp.clip(drawn, -reach, reach).astype(held_as)


def setup_inputs(seed: int = 0) -> dict:
    seeds = jax.random.split(jax.random.key(seed), 12)
    return {
        "frames": noise(seeds[0], (FRAMES, GRID_ROWS, GRID_COLS, D), 1.0, 6.0, ((0, 8), (1, 4))),
        "token_ids": set_ends(jax.random.randint(seeds[1], (STEPS, FRAMES, GRID_ROWS, GRID_COLS), 0, VOCAB), jax.random.fold_in(seeds[1], 1), 0, VOCAB - 1).astype(jnp.int32),
        "action_ids": set_ends(jax.random.randint(seeds[2], (FRAMES,), 0, ACTIONS), jax.random.fold_in(seeds[2], 1), 0, ACTIONS - 1).astype(jnp.int32),
        "token_table": noise(seeds[3], (VOCAB, D), 1.0, 6.0),
        "action_table": noise(seeds[4], (ACTIONS, D), 0.5, 3.0),
        "conv_weight": noise(seeds[5], (3, 3, D), 0.3, 1.796875),
        "norm_gain": jnp.clip(1.0 + 0.1 * jax.random.normal(seeds[6], (D,), jnp.float32), 0.5, 1.5).astype(jnp.bfloat16),
        "w_query": draw_w_query(jax.random.fold_in(seeds[11], 71), 0),
        "w_key": draw_w_key(jax.random.fold_in(seeds[11], 71), 0),
        "w_value": noise(seeds[9], (D, D), D ** -0.5, 0.3125),
        "w_out": noise(seeds[10], (D, D), (D // 4) ** -0.5, 0.625),
    }


def attend(queries, keys, values, first_frame, head_count):
    frame_count, positions, width_all = queries.shape
    head_dim = width_all // head_count
    query_frame = first_frame + jnp.arange(frame_count, dtype=jnp.int32)
    key_frame = jnp.concatenate([first_frame - (WINDOW - 1) + jnp.arange(WINDOW - 1 + frame_count, dtype=jnp.int32), jnp.arange(ANCHORS, dtype=jnp.int32)])
    is_anchor = jnp.arange(key_frame.shape[0]) >= WINDOW - 1 + frame_count
    lower = query_frame[:, None] - (WINDOW - 1)
    in_window = (key_frame[None, :] >= 0) & (key_frame[None, :] <= query_frame[:, None]) & (key_frame[None, :] >= lower)
    allowed = jnp.where(is_anchor[None, :], key_frame[None, :] < lower, in_window)
    query_heads = queries.reshape(frame_count, positions, head_count, head_dim).astype(jnp.float32)
    key_heads = keys.reshape(keys.shape[0], positions, head_count, head_dim).astype(jnp.float32)
    value_heads = values.reshape(values.shape[0], positions, head_count, head_dim).astype(jnp.float32)
    scores = jnp.einsum('fphd,kphd->phfk', query_heads, key_heads) / jnp.sqrt(jnp.float32(head_dim))
    scores = jnp.where(allowed[None, None], scores, jnp.float32(-1e+30))
    row_max = lax.optimization_barrier(jnp.max(scores, axis=-1, keepdims=True))
    expo = jnp.exp(scores - row_max)
    probs = (expo / lax.optimization_barrier(jnp.sum(expo, axis=-1, keepdims=True))).astype(jnp.bfloat16)
    attended = jnp.einsum('phfk,kphd->fphd', probs.astype(jnp.float32), value_heads)
    return attended.reshape(frame_count, positions, width_all).astype(jnp.bfloat16)

def reference(frames, token_ids, action_ids, token_table, action_table, conv_weight, norm_gain, w_query, w_key, w_value, w_out):
    frame_total, row_count, col_count, width_all = frames.shape
    positions = row_count * col_count
    onehot = (action_ids[:, None] == jnp.arange(ACTIONS, dtype=jnp.int32)[None, :]).astype(jnp.bfloat16)
    action_rows = jnp.dot(onehot, action_table, preferred_element_type=jnp.float32)
    state = frames
    block_count = frame_total // FR_DEV
    for step_index in range(STEPS):
        token_rows = token_table[token_ids[step_index]]
        embedded = (state.astype(jnp.float32) + token_rows.astype(jnp.float32) + action_rows[:, None, None, :]).astype(jnp.bfloat16)
        padded = jnp.pad(embedded, ((0, 0), (1, 1), (1, 1), (0, 0)))
        mixed = embedded.astype(jnp.float32)
        for row_shift in range(3):
            for col_shift in range(3):
                mixed = mixed + padded[:, row_shift:row_shift + row_count, col_shift:col_shift + col_count, :].astype(jnp.float32) * conv_weight[row_shift, col_shift].astype(jnp.float32)
        scale = lax.rsqrt(lax.optimization_barrier(jnp.mean(mixed * mixed, axis=-1, keepdims=True)) + 1e-06)
        normed = (mixed * scale * norm_gain.astype(jnp.float32)).astype(jnp.bfloat16)
        flat = normed.reshape(frame_total * positions, width_all)
        queries = jnp.dot(flat, w_query, preferred_element_type=jnp.float32).astype(jnp.bfloat16).reshape(frame_total, positions, width_all)
        keys = jnp.dot(flat, w_key, preferred_element_type=jnp.float32).astype(jnp.bfloat16).reshape(frame_total, positions, width_all)
        values = jnp.dot(flat, w_value, preferred_element_type=jnp.float32).astype(jnp.bfloat16).reshape(frame_total, positions, width_all)
        keys_padded = jnp.pad(keys, ((WINDOW - 1, 0), (0, 0), (0, 0)))
        values_padded = jnp.pad(values, ((WINDOW - 1, 0), (0, 0), (0, 0)))

        def one_block(block_index):
            first_frame = (block_index * FR_DEV).astype(jnp.int32)
            query_block = lax.dynamic_slice_in_dim(queries, first_frame, FR_DEV, 0)
            key_block = lax.dynamic_slice_in_dim(keys_padded, first_frame, FR_DEV + WINDOW - 1, 0)
            value_block = lax.dynamic_slice_in_dim(values_padded, first_frame, FR_DEV + WINDOW - 1, 0)
            key_block = jnp.concatenate([key_block, keys[:ANCHORS]], axis=0)
            value_block = jnp.concatenate([value_block, values[:ANCHORS]], axis=0)
            return attend(query_block, key_block, value_block, first_frame, HEADS)
        attended = lax.map(one_block, jnp.arange(block_count, dtype=jnp.int32))
        attended = attended.reshape(frame_total * positions, width_all)
        output = jnp.dot(attended, w_out, preferred_element_type=jnp.float32).reshape(frame_total, row_count, col_count, width_all)
        state = (mixed + output).astype(jnp.bfloat16)
    return state
```

```python
import jax
import jax.numpy as jnp
from jax import lax
from jax.experimental import pallas as pl
from jax.experimental.pallas import tpu as pltpu
from jax.sharding import PartitionSpec as P

HEADS = 6
ACTIONS = 8
WINDOW = 16
ANCHORS = 4
GROUP = 16
F32 = jnp.float32
BF16 = jnp.bfloat16
NT = (((1,), (1,)), ((), ()))
VMEM_LIMIT = 48 * 1024 * 1024


def shift_cols(y, by):
    cols = y.shape[0]
    rolled = pltpu.roll(y, by % cols, 0)
    at = lax.broadcasted_iota(jnp.int32, y.shape, 0)
    edge = 0 if by == 1 else cols - 1
    return jnp.where(at == edge, 0.0, rolled)


def conv_norm(above, here, below, conv, gain):
    rows = [r.astype(F32) for r in (above, here, below)]
    sums = []
    for j in range(3):
        sums.append(
            rows[0] * conv[j : j + 1]
            + rows[1] * conv[3 + j : 4 + j]
            + rows[2] * conv[6 + j : 7 + j]
        )
    mixed = rows[1] + sums[1] + shift_cols(sums[0], 1) + shift_cols(sums[2], -1)
    scale = lax.rsqrt(jnp.mean(mixed * mixed, axis=-1, keepdims=True) + 1e-06)
    return mixed, (mixed * scale * gain).astype(BF16)


def embed_kernel(
    ids, frames, actions, table, conv_ref, gain_ref, emb, top, bottom, mixed, normed
):
    f = pl.program_id(0)
    row_count, cols, width = frames.shape[1:]
    vocab = table.shape[0]
    action = actions[pl.ds(f, 1), :]
    codes = lax.broadcasted_iota(jnp.int32, (cols, vocab), 1)
    rows = []
    for r in range(row_count):
        onehot = jnp.where(codes == ids[r * cols : (r + 1) * cols, :], 1.0, 0.0).astype(BF16)
        token = jnp.dot(onehot, table[...], preferred_element_type=F32)
        row = (frames[0, r].astype(F32) + token + action).astype(BF16)
        emb[0, r] = row
        rows.append(row)
    top[0] = rows[0]
    bottom[0] = rows[-1]
    conv = conv_ref[...]
    gain = gain_ref[...]
    for r in range(1, row_count - 1):
        m, n = conv_norm(rows[r - 1], rows[r], rows[r + 1], conv, gain)
        mixed[0, (r - 1) * cols : r * cols, :] = m
        normed[0, (r - 1) * cols : r * cols, :] = n


def edge_kernel(emb, before, after, conv_ref, gain_ref, mixed, normed):
    row_count, cols = emb.shape[1:3]
    conv = conv_ref[...]
    gain = gain_ref[...]
    m, n = conv_norm(before[0], emb[0, 0], emb[0, 1], conv, gain)
    mixed[0, :cols, :] = m
    normed[0, :cols, :] = n
    m, n = conv_norm(emb[0, row_count - 2], emb[0, row_count - 1], after[0], conv, gain)
    mixed[0, cols:, :] = m
    normed[0, cols:, :] = n


def attend_kernel(
    tm_ref, own, prev_lo, prev_hi, anchors, mixed, w_qkv, w_out, *rest
):
    out = rest[-1]
    tm = tm_ref[0]
    frame_count, group, width = own.shape
    rows = frame_count * group
    anchor_rows = ANCHORS * group
    x = own[...].reshape(rows, width)
    before = jnp.concatenate([prev_lo[...], prev_hi[...]], axis=0).reshape(rows, width)
    first = anchors[...].reshape(anchor_rows, width)
    qkv = jnp.dot(x, w_qkv[...], preferred_element_type=F32)
    q = (qkv[:, :width].astype(BF16) * 0.125).astype(BF16)
    kv_own = qkv[:, width:].astype(BF16)
    kv_prev = jnp.dot(before, w_qkv[:, width:], preferred_element_type=F32).astype(BF16)
    kv_anchor = jnp.dot(first, w_qkv[:, width:], preferred_element_type=F32).astype(BF16)

    at_q = lax.broadcasted_iota(jnp.int32, (rows, rows), 0)
    at_k = lax.broadcasted_iota(jnp.int32, (rows, rows), 1)
    causal = at_k // group <= at_q // group
    same = at_k % group == at_q % group
    bias = jnp.where(same & (causal | (tm > 0)), 0.0, -1e30)
    at_q = lax.broadcasted_iota(jnp.int32, (rows, anchor_rows), 0)
    at_k = lax.broadcasted_iota(jnp.int32, (rows, anchor_rows), 1)
    limit = tm * frame_count + at_q // group - (WINDOW - 1)
    seen = (at_k % group == at_q % group) & (at_k // group < limit)
    anchor_bias = jnp.where(seen, 0.0, -1e30)

    lane = lax.broadcasted_iota(jnp.int32, (rows, 128), 1)
    parts = []
    for pair in range(width // 128):
        at = slice(pair * 128, (pair + 1) * 128)
        at_v = slice(width + pair * 128, width + (pair + 1) * 128)
        halves = []
        for half in range(2):
            mine = (lane < 64) if half == 0 else (lane >= 64)
            qh = jnp.where(mine, q[:, at], jnp.zeros((), BF16))
            s_own = lax.dot_general(qh, kv_own[:, at], NT, preferred_element_type=F32)
            s_prev = lax.dot_general(qh, kv_prev[:, at], NT, preferred_element_type=F32)
            s_first = lax.dot_general(qh, kv_anchor[:, at], NT, preferred_element_type=F32)
            s = jnp.where(causal, s_own, s_prev) + bias
            s_first = s_first + anchor_bias
            top = jnp.maximum(
                jnp.max(s, axis=-1, keepdims=True), jnp.max(s_first, axis=-1, keepdims=True)
            )
            e = jnp.exp(s - top)
            e_first = jnp.exp(s_first - top)
            total = jnp.sum(e, axis=-1, keepdims=True) + jnp.sum(
                e_first, axis=-1, keepdims=True
            )
            e_own = jnp.where(causal, e, 0.0).astype(BF16)
            e_prev = jnp.where(causal, 0.0, e).astype(BF16)
            o = jnp.dot(e_own, kv_own[:, at_v], preferred_element_type=F32)
            o += jnp.dot(e_prev, kv_prev[:, at_v], preferred_element_type=F32)
            o += jnp.dot(
                e_first.astype(BF16), kv_anchor[:, at_v], preferred_element_type=F32
            )
            halves.append(o / total)
        parts.append(jnp.where(lane < 64, halves[0], halves[1]).astype(BF16))
    attended = jnp.concatenate(parts, axis=1)
    result = jnp.dot(attended, w_out[...], preferred_element_type=F32)
    result = result.reshape(frame_count, group, width) + mixed[...]
    out[...] = result.astype(BF16).reshape(out.shape)


def params():
    return pltpu.CompilerParams(vmem_limit_bytes=VMEM_LIMIT)


def embed(ids, frames, actions, table, conv, gain):
    count, row_count, cols, width = frames.shape
    strip = jax.ShapeDtypeStruct((count, cols, width), BF16)
    inner = (row_count - 2) * cols
    strip_spec = pl.BlockSpec((1, cols, width), lambda f: (f, 0, 0))
    inner_spec = pl.BlockSpec((1, inner, width), lambda f: (f, 0, 0))
    frame_spec = pl.BlockSpec((1, row_count, cols, width), lambda f: (f, 0, 0, 0))

    def whole(a):
        return pl.BlockSpec(a.shape, lambda f: (0,) * a.ndim)

    return pl.pallas_call(
        embed_kernel,
        grid=(count,),
        in_specs=[
            pl.BlockSpec((row_count * cols, 1), lambda f: (f, 0)),
            frame_spec,
            whole(actions),
            whole(table),
            whole(conv),
            whole(gain),
        ],
        out_specs=[frame_spec, strip_spec, strip_spec, inner_spec, inner_spec],
        out_shape=[
            jax.ShapeDtypeStruct(frames.shape, BF16),
            strip,
            strip,
            jax.ShapeDtypeStruct((count, inner, width), F32),
            jax.ShapeDtypeStruct((count, inner, width), BF16),
        ],
        compiler_params=params(),
        cost_estimate=pl.CostEstimate(
            flops=2 * ids.shape[0] * table.shape[0] * width,
            bytes_accessed=16 * 1024 * 1024,
            transcendentals=0,
        ),
        name="embed",
    )(ids, frames, actions, table, conv, gain)


def edge(emb, before, after, conv, gain):
    count, row_count, cols, width = emb.shape
    strip_spec = pl.BlockSpec((1, cols, width), lambda f: (f, 0, 0))
    edge_spec = pl.BlockSpec((1, 2 * cols, width), lambda f: (f, 0, 0))
    frame_spec = pl.BlockSpec((1, row_count, cols, width), lambda f: (f, 0, 0, 0))

    def whole(a):
        return pl.BlockSpec(a.shape, lambda f: (0,) * a.ndim)

    return pl.pallas_call(
        edge_kernel,
        grid=(count,),
        in_specs=[frame_spec, strip_spec, strip_spec, whole(conv), whole(gain)],
        out_specs=[edge_spec, edge_spec],
        out_shape=[
            jax.ShapeDtypeStruct((count, 2 * cols, width), F32),
            jax.ShapeDtypeStruct((count, 2 * cols, width), BF16),
        ],
        compiler_params=params(),
        cost_estimate=pl.CostEstimate(
            flops=20 * emb.size, bytes_accessed=16 * 1024 * 1024, transcendentals=0
        ),
        name="edge",
    )(emb, before, after, conv, gain)


def attend(tm, own, prev_lo, prev_hi, anchors, mixed, w_qkv, w_out, out, shape, row_of):
    count, positions, width = own.shape
    cols = shape[2]
    per_row = cols // GROUP

    def block(a):
        return pl.BlockSpec((a.shape[0], GROUP, width), lambda g: (0, g, 0))

    def whole(a):
        return pl.BlockSpec(a.shape, lambda g: (0, 0))

    args = [tm, own, prev_lo, prev_hi, anchors, mixed, w_qkv, w_out]
    specs = [pl.BlockSpec(memory_space=pltpu.SMEM)]
    specs += [block(a) for a in args[1:6]] + [whole(w_qkv), whole(w_out)]
    aliases = {}
    if out is not None:
        aliases = {len(args): 0}
        args.append(out)
        specs.append(pl.BlockSpec(memory_space=pl.ANY))
    return pl.pallas_call(
        attend_kernel,
        grid=(positions // GROUP,),
        in_specs=specs,
        out_specs=pl.BlockSpec(
            (count, 1, GROUP, width), lambda g: (0, row_of(g // per_row), g % per_row, 0)
        ),
        out_shape=jax.ShapeDtypeStruct(shape, BF16),
        input_output_aliases=aliases,
        compiler_params=params(),
        cost_estimate=pl.CostEstimate(
            flops=16_000_000_000, bytes_accessed=16 * 1024 * 1024, transcendentals=0
        ),
        name="attend",
    )(*args)


def send(x, by):
    count = lax.axis_size("tm")
    return lax.ppermute(x, "tm", [(i, i + by) for i in range(count - by)])


def window_of(normed, tm):
    count = lax.axis_size("tm")
    lo = send(normed[:ANCHORS], 1)
    hi = send(normed[ANCHORS:], 1)
    anchors = jnp.where(tm == 0, normed[:ANCHORS], lo)
    by = count // 2
    while by >= 2:
        pairs = [(i, i + by) for i in range(count - by) if i % (2 * by) < 2]
        got = lax.ppermute(anchors, "tm", pairs)
        place = tm % (2 * by)
        anchors = jnp.where((place == by) | (place == by + 1), got, anchors)
        by //= 2
    return lo, hi, anchors


def on_device(
    frames,
    token_ids,
    action_ids,
    token_table,
    action_table,
    conv_weight,
    norm_gain,
    w_query,
    w_key,
    w_value,
    w_out,
):
    shape = frames.shape
    width = shape[3]
    tm = lax.axis_index("tm")
    tm_arg = tm.astype(jnp.int32).reshape(1)
    ids = token_ids[0].reshape(-1, 1)
    onehot = (action_ids[:, None] == jnp.arange(ACTIONS, dtype=jnp.int32)[None, :]).astype(BF16)
    actions = jnp.dot(onehot, action_table, preferred_element_type=F32)
    conv = conv_weight.reshape(9, width).astype(F32)
    gain = norm_gain.reshape(1, width).astype(F32)
    w_qkv = jnp.concatenate([w_query, w_key, w_value], axis=1)

    emb, top, bottom, mixed_in, normed_in = embed(ids, frames, actions, token_table, conv, gain)
    strips = lax.axis_size("space")
    up = [(i, i + 1) for i in range(strips - 1)]
    before = lax.ppermute(bottom, "space", up)
    after = lax.ppermute(top, "space", [(j, i) for i, j in up])
    sent_in = window_of(normed_in, tm)
    mixed_edge, normed_edge = edge(emb, before, after, conv, gain)
    sent_edge = window_of(normed_edge, tm)
    last = shape[1] - 1
    out = attend(
        tm_arg, normed_in, *sent_in, mixed_in, w_qkv, w_out, None, shape, lambda r: r + 1
    )
    return attend(
        tm_arg, normed_edge, *sent_edge, mixed_edge, w_qkv, w_out, out, shape, lambda r: r * last
    )


def solution(mesh):
    in_specs = (
        P("tm", "space", None, None),
        P(None, "tm", "space", None),
        P("tm"),
        P(),
        P(),
        P(),
        P(),
        P(),
        P(),
        P(),
        P(),
    )
    out_specs = P("tm", "space", None, None)
    return jax.shard_map(
        on_device, mesh=mesh, in_specs=in_specs, out_specs=out_specs, check_vma=False
    )
```

```python
import jax
import jax.numpy as jnp
from jax import lax
from jax.experimental import pallas as pl
from jax.experimental.pallas import tpu as pltpu
from jax.sharding import PartitionSpec as P

HEADS = 6
ACTIONS = 8
WINDOW = 16
ANCHORS = 4
GROUP = 8
F32 = jnp.float32
BF16 = jnp.bfloat16
NT = (((1,), (1,)), ((), ()))
TN = (((0,), (0,)), ((), ()))
VMEM_LIMIT = 48 * 1024 * 1024


def shift_cols(y, by):
    cols = y.shape[0]
    rolled = pltpu.roll(y, by % cols, 0)
    at = lax.broadcasted_iota(jnp.int32, y.shape, 0)
    edge = 0 if by == 1 else cols - 1
    return jnp.where(at == edge, 0.0, rolled)


def conv_norm(above, here, below, conv, gain):
    rows = [r.astype(F32) for r in (above, here, below)]
    sums = []
    for j in range(3):
        sums.append(
            rows[0] * conv[j : j + 1]
            + rows[1] * conv[3 + j : 4 + j]
            + rows[2] * conv[6 + j : 7 + j]
        )
    mixed = rows[1] + sums[1] + shift_cols(sums[0], 1) + shift_cols(sums[2], -1)
    scale = lax.rsqrt(jnp.mean(mixed * mixed, axis=-1, keepdims=True) + 1e-06)
    return mixed, mixed * scale * gain


def grouped(first, second):
    width = first.shape[-1]
    first = first.reshape(-1, GROUP, width)
    second = second.reshape(-1, GROUP, width)
    return jnp.concatenate([first, second], axis=1)


def put_rows(results, mixed, normed, rolled):
    frame = pl.program_id(0) * 2
    turned = []
    for k in range(2):
        n = results[k][1].reshape(-1, GROUP, results[k][1].shape[-1])
        turned.append(pltpu.roll(n, lax.rem(frame + k, GROUP), 1))
    mixed[...] = grouped(results[0][0], results[1][0])
    normed[...] = grouped(results[0][1], results[1][1]).astype(BF16)
    rolled[...] = jnp.concatenate(turned, axis=1).astype(BF16)


def embed_kernel(
    ids, frames, actions, table, conv_ref, gain_ref, emb, top, bottom, mixed, normed, rolled
):
    step = pl.program_id(0)
    row_count, cols, width = frames.shape[1:]
    vocab = table.shape[0]
    count = 2 * row_count * cols
    row_ids = ids[0].astype(F32)
    codes = jnp.transpose(jnp.broadcast_to(row_ids, (128, count)), (1, 0))
    lane = lax.broadcasted_iota(jnp.int32, (count, 128), 1).astype(F32)
    onehot = [
        jnp.where(codes == lane + 128.0 * k, 1.0, 0.0).astype(BF16) for k in range(vocab // 128)
    ]
    tokens = jnp.dot(jnp.concatenate(onehot, axis=1), table[...], preferred_element_type=F32)
    conv = conv_ref[...]
    gain = gain_ref[...]
    results = []
    for k in range(2):
        action = actions[pl.ds(step * 2 + k, 1), :]
        rows = []
        for r in range(row_count):
            at = (k * row_count + r) * cols
            row = frames[k, r].astype(F32) + tokens[at : at + cols] + action
            row = row.astype(BF16)
            emb[k, r] = row
            rows.append(row)
        top[k] = rows[0]
        bottom[k] = rows[-1]
        done = [
            conv_norm(rows[r - 1], rows[r], rows[r + 1], conv, gain)
            for r in range(1, row_count - 1)
        ]
        results.append([jnp.concatenate(part, axis=0) for part in zip(*done)])
    put_rows(results, mixed, normed, rolled)


def edge_kernel(emb, before, after, conv_ref, gain_ref, mixed, normed, rolled):
    row_count = emb.shape[1]
    conv = conv_ref[...]
    gain = gain_ref[...]
    results = []
    for k in range(2):
        done = [
            conv_norm(before[k], emb[k, 0], emb[k, 1], conv, gain),
            conv_norm(emb[k, row_count - 2], emb[k, row_count - 1], after[k], conv, gain),
        ]
        results.append([jnp.concatenate(part, axis=0) for part in zip(*done)])
    put_rows(results, mixed, normed, rolled)


def attend_kernel(
    tm_ref, x_ref, own, lo, hi, anchors, mixed, wq_t, wk, wv_t, w_out, *rest
):
    out, mask = rest[-2:]
    tm = tm_ref[0]
    width = x_ref.shape[-1]
    queries = WINDOW * GROUP
    lanes = 2 * queries
    slabs = 2 * WINDOW + ANCHORS

    @pl.when(pl.program_id(0) == 0)
    def _():
        row = lax.broadcasted_iota(jnp.int32, (slabs * GROUP, lanes), 0)
        lane = lax.broadcasted_iota(jnp.int32, (slabs * GROUP, lanes), 1)
        u = row // GROUP
        t = (lane % queries) // GROUP
        met = (row - lane + lanes) % GROUP
        mine = (u < WINDOW) & (u % GROUP == met) & (u <= t)
        past = (u >= WINDOW) & (u < 2 * WINDOW) & (u % GROUP == met) & (u - WINDOW > t)
        first = (u >= 2 * WINDOW) & (u - 2 * WINDOW == met)
        mask[...] = jnp.where(mine | past | first, 1.0, 0.0).astype(BF16)

    sub = lax.broadcasted_iota(jnp.int32, (GROUP, lanes), 0)
    lane = lax.broadcasted_iota(jnp.int32, (GROUP, lanes), 1)
    t = (lane % queries) // GROUP
    met = (sub - lane + lanes) % GROUP
    places = []
    for b in range(WINDOW // GROUP):
        u = met + b * GROUP
        places.append(jnp.where(u <= t, u, u + WINDOW))
    open_window = [(c < WINDOW) | (tm > 0) for c in places]
    open_anchor = (met < ANCHORS) & (met < tm * WINDOW + t - (WINDOW - 1))

    x = x_ref[...].reshape(-1, width)
    q_t = lax.dot_general(wq_t[...], x, NT, preferred_element_type=F32).astype(BF16)
    q_t = (q_t * 0.125).astype(BF16)
    anchor_rows = ANCHORS * GROUP
    va_t = lax.dot_general(
        wv_t[...], anchors[...].reshape(2 * anchor_rows, width), NT, preferred_element_type=F32
    ).astype(BF16)
    blank = jnp.zeros((64, queries), BF16)
    no_rows = jnp.zeros((anchor_rows, lanes), BF16)
    results = []
    for i in range(2):
        window = jnp.concatenate([own[i], lo[i], hi[i]], axis=0)
        keys = jnp.concatenate([window, anchors[i]], axis=0)
        k = jnp.dot(keys, wk[...], preferred_element_type=F32).astype(BF16)
        v_t = lax.dot_general(wv_t[...], window, NT, preferred_element_type=F32).astype(BF16)
        parts = []
        for pair in range(width // 128):
            at = pair * 128
            across = slice(i * queries, (i + 1) * queries)
            left = jnp.concatenate([q_t[at : at + 64, across], blank], axis=0)
            right = jnp.concatenate([blank, q_t[at + 64 : at + 128, across]], axis=0)
            s = jnp.dot(
                k[:, at : at + 128],
                jnp.concatenate([left, right], axis=1),
                preferred_element_type=F32,
            )
            s = [s[j * GROUP : (j + 1) * GROUP] for j in range(slabs)]
            merged = []
            for b in range(WINDOW // GROUP):
                w = s[b * GROUP]
                for d in range(GROUP):
                    u = b * GROUP + d
                    if d > 0:
                        w = jnp.where(places[b] == u, s[u], w)
                    w = jnp.where(places[b] == WINDOW + u, s[WINDOW + u], w)
                merged.append(jnp.where(open_window[b], w, -1e30))
            w = s[2 * WINDOW]
            for u in range(1, ANCHORS):
                w = jnp.where(met == u, s[2 * WINDOW + u], w)
            merged.append(jnp.where(open_anchor, w, -1e30))
            top = jnp.max(
                jnp.maximum(jnp.maximum(merged[0], merged[1]), merged[2]), axis=0, keepdims=True
            )
            e = [jnp.exp(w - top) for w in merged]
            total = jnp.sum(e[0] + e[1] + e[2], axis=0, keepdims=True)
            over = 1.0 / total
            p = [w * over for w in e]
            p = [jnp.concatenate([w, w], axis=0).astype(BF16) for w in p]
            spread = []
            for j in range(slabs // 2):
                b = (2 * j % WINDOW) // GROUP if j < WINDOW else 2
                spread.append(p[b] * mask[j * 16 : (j + 1) * 16, :])
            p_window = jnp.concatenate(spread[:WINDOW], axis=0)
            p_first = jnp.concatenate(spread[WINDOW:], axis=0)
            p_first = [p_first, no_rows] if i == 0 else [no_rows, p_first]
            o = jnp.dot(v_t[at : at + 128], p_window, preferred_element_type=F32)
            o += jnp.dot(
                va_t[at : at + 128],
                jnp.concatenate(p_first, axis=0),
                preferred_element_type=F32,
            )
            parts += [o[:64, :queries], o[64:, queries:]]
        attended = jnp.concatenate(parts, axis=0).astype(BF16)
        result = lax.dot_general(attended, w_out[...], TN, preferred_element_type=F32)
        results.append((result + mixed[i]).reshape(WINDOW, GROUP, width))
    out[...] = jnp.concatenate(results, axis=1).astype(BF16).reshape(out.shape)


def params():
    return pltpu.CompilerParams(vmem_limit_bytes=VMEM_LIMIT)


def small():
    return pl.CostEstimate(flops=1000, bytes_accessed=1000, transcendentals=0)


def whole(a):
    return pl.BlockSpec(a.shape, lambda f: (0,) * a.ndim)


def row_outputs(count, positions, width):
    groups = positions // GROUP
    spec = pl.BlockSpec((groups, 2 * GROUP, width), lambda f: (0, f, 0))
    shapes = [
        jax.ShapeDtypeStruct((groups, count * GROUP, width), dtype) for dtype in (F32, BF16, BF16)
    ]
    return [spec] * 3, shapes


def embed(ids, frames, actions, table, conv, gain):
    count, row_count, cols, width = frames.shape
    strip = jax.ShapeDtypeStruct((count, cols, width), BF16)
    strip_spec = pl.BlockSpec((2, cols, width), lambda f: (f, 0, 0))
    frame_spec = pl.BlockSpec((2, row_count, cols, width), lambda f: (f, 0, 0, 0))
    specs, shapes = row_outputs(count, (row_count - 2) * cols, width)
    return pl.pallas_call(
        embed_kernel,
        grid=(count // 2,),
        in_specs=[
            pl.BlockSpec((1, 1, 2 * row_count * cols), lambda f: (f, 0, 0)),
            frame_spec,
            whole(actions),
            whole(table),
            whole(conv),
            whole(gain),
        ],
        out_specs=[frame_spec, strip_spec, strip_spec] + specs,
        out_shape=[jax.ShapeDtypeStruct(frames.shape, BF16), strip, strip] + shapes,
        compiler_params=params(),
        cost_estimate=small(),
        name="embed",
    )(ids, frames, actions, table, conv, gain)


def edge(emb, before, after, conv, gain):
    count, row_count, cols, width = emb.shape
    strip_spec = pl.BlockSpec((2, cols, width), lambda f: (f, 0, 0))
    frame_spec = pl.BlockSpec((2, row_count, cols, width), lambda f: (f, 0, 0, 0))
    specs, shapes = row_outputs(count, 2 * cols, width)
    return pl.pallas_call(
        edge_kernel,
        grid=(count // 2,),
        in_specs=[frame_spec, strip_spec, strip_spec, whole(conv), whole(gain)],
        out_specs=specs,
        out_shape=shapes,
        compiler_params=params(),
        cost_estimate=small(),
        name="edge",
    )(emb, before, after, conv, gain)


def attend(tm, blocks, weights, out, shape, row_of):
    count, _, cols, width = shape
    positions = blocks[0].shape[0] * GROUP
    per_row = cols // (2 * GROUP)

    def block(a):
        return pl.BlockSpec((2,) + a.shape[1:], lambda g: (g, 0, 0))

    args = [tm, *blocks, *weights]
    specs = [pl.BlockSpec(memory_space=pltpu.SMEM)]
    specs += [block(a) for a in blocks] + [whole(w) for w in weights]
    aliases = {}
    if out is not None:
        aliases = {len(args): 0}
        args.append(out)
        specs.append(pl.BlockSpec(memory_space=pl.ANY))
    return pl.pallas_call(
        attend_kernel,
        grid=(positions // (2 * GROUP),),
        in_specs=specs,
        out_specs=pl.BlockSpec(
            (count, 1, 2 * GROUP, width), lambda g: (0, row_of(g // per_row), g % per_row, 0)
        ),
        out_shape=jax.ShapeDtypeStruct(shape, BF16),
        scratch_shapes=[
            pltpu.VMEM(((2 * WINDOW + ANCHORS) * GROUP, 2 * WINDOW * GROUP), BF16)
        ],
        input_output_aliases=aliases,
        compiler_params=params(),
        cost_estimate=small(),
        name="attend",
    )(*args)


def send(x, by):
    count = lax.axis_size("tm")
    return lax.ppermute(x, "tm", [(i, i + by) for i in range(count - by)])


def window_of(normed, tm, after=None):
    count = lax.axis_size("tm")
    first = normed[:, : ANCHORS * GROUP]
    if after is not None:
        first, after = lax.optimization_barrier((first, after))
    lo = send(first, 1)
    hi = send(normed[:, ANCHORS * GROUP :], 1)
    anchors = jnp.where(tm == 0, first, lo)
    by = count // 2
    while by >= 2:
        pairs = [(i, i + by) for i in range(count - by) if i % (2 * by) < 2]
        got = lax.ppermute(anchors, "tm", pairs)
        place = tm % (2 * by)
        anchors = jnp.where((place == by) | (place == by + 1), got, anchors)
        by //= 2
    return lo, hi, anchors


def on_device(
    frames,
    token_ids,
    action_ids,
    token_table,
    action_table,
    conv_weight,
    norm_gain,
    w_query,
    w_key,
    w_value,
    w_out,
):
    shape = frames.shape
    width = shape[3]
    tm = lax.axis_index("tm")
    tm_arg = tm.astype(jnp.int32).reshape(1)
    ids = token_ids.reshape(shape[0] // 2, 1, -1)
    onehot = (action_ids[:, None] == jnp.arange(ACTIONS, dtype=jnp.int32)[None, :]).astype(BF16)
    actions = jnp.dot(onehot, action_table, preferred_element_type=F32)
    conv = conv_weight.reshape(9, width).astype(F32)
    gain = norm_gain.reshape(1, width).astype(F32)
    weights = [w_query.T, w_key, w_value.T, w_out]

    emb, top, bottom, mixed, normed, rolled = embed(ids, frames, actions, token_table, conv, gain)
    strips = lax.axis_size("space")
    up = [(i, i + 1) for i in range(strips - 1)]
    before = lax.ppermute(bottom, "space", up)
    after = lax.ppermute(top, "space", [(j, i) for i, j in up])
    lo, hi, anchors = window_of(rolled, tm)
    inner = [normed, rolled, lo, hi, anchors, mixed]
    mixed, normed, rolled = edge(emb, before, after, conv, gain)
    outer = [normed, rolled, *window_of(rolled, tm, hi), mixed]
    last = shape[1] - 1
    out = attend(tm_arg, inner, weights, None, shape, lambda r: r + 1)
    return attend(tm_arg, outer, weights, out, shape, lambda r: r * last)


def solution(mesh):
    in_specs = (
        P("tm", "space", None, None),
        P(None, "tm", "space", None),
        P("tm"),
        P(),
        P(),
        P(),
        P(),
        P(),
        P(),
        P(),
        P(),
    )
    out_specs = P("tm", "space", None, None)
    return jax.shard_map(
        on_device, mesh=mesh, in_specs=in_specs, out_specs=out_specs, check_vma=False
    )
```

```python
import functools

import jax
import jax.numpy as jnp
from jax import lax
from jax.experimental import pallas as pl
from jax.experimental.pallas import tpu as pltpu
from jax.sharding import PartitionSpec as P

HEADS = 6
ACTIONS = 8
WINDOW = 16
ANCHORS = 4
GROUP = 8
STEP = 4
F32 = jnp.float32
BF16 = jnp.bfloat16
NT = (((1,), (1,)), ((), ()))
TN = (((0,), (0,)), ((), ()))
VMEM_LIMIT = 48 * 1024 * 1024


def shift_cols(y, by):
    cols = y.shape[0]
    rolled = pltpu.roll(y, by % cols, 0)
    at = lax.broadcasted_iota(jnp.int32, y.shape, 0)
    edge = 0 if by == 1 else cols - 1
    return jnp.where(at == edge, 0.0, rolled)


def conv_norm(above, here, below, conv, gain):
    rows = [r.astype(F32) for r in (above, here, below)]
    sums = []
    for j in range(3):
        sums.append(
            rows[0] * conv[j : j + 1]
            + rows[1] * conv[3 + j : 4 + j]
            + rows[2] * conv[6 + j : 7 + j]
        )
    mixed = rows[1] + sums[1] + shift_cols(sums[0], 1) + shift_cols(sums[2], -1)
    scale = lax.rsqrt(jnp.mean(mixed * mixed, axis=-1, keepdims=True) + 1e-06)
    return mixed, mixed * scale * gain


def grouped(first, second):
    width = first.shape[-1]
    first = first.reshape(-1, GROUP, width)
    second = second.reshape(-1, GROUP, width)
    return jnp.concatenate([first, second], axis=1)


def put_rows(first, results, mixed, normed, rolled):
    frame = pl.program_id(0) * 2 + first
    turned = []
    for k in range(2):
        n = results[k][1].reshape(-1, GROUP, results[k][1].shape[-1])
        turned.append(pltpu.roll(n, lax.rem(frame + k, GROUP), 1))
    mixed[...] = grouped(results[0][0], results[1][0])
    normed[...] = grouped(results[0][1], results[1][1]).astype(BF16)
    rolled[...] = jnp.concatenate(turned, axis=1).astype(BF16)


def embed_kernel(
    first, ids, frames, actions, table, conv_ref, gain_ref, emb, top, bottom, mixed, normed, rolled
):
    frame = pl.program_id(0) * 2 + first
    row_count, cols, width = frames.shape[1:]
    vocab = table.shape[0]
    count = 2 * row_count * cols
    row_ids = ids[0].astype(F32)
    codes = jnp.transpose(jnp.broadcast_to(row_ids, (128, count)), (1, 0))
    lane = lax.broadcasted_iota(jnp.int32, (count, 128), 1).astype(F32)
    onehot = [
        jnp.where(codes == lane + 128.0 * k, 1.0, 0.0).astype(BF16) for k in range(vocab // 128)
    ]
    tokens = jnp.dot(jnp.concatenate(onehot, axis=1), table[...], preferred_element_type=F32)
    conv = conv_ref[...]
    gain = gain_ref[...]
    results = []
    for k in range(2):
        action = actions[pl.ds(frame + k, 1), :]
        rows = []
        for r in range(row_count):
            at = (k * row_count + r) * cols
            row = frames[k, r].astype(F32) + tokens[at : at + cols] + action
            row = row.astype(BF16)
            emb[k, r] = row
            rows.append(row)
        top[k] = rows[0]
        bottom[k] = rows[-1]
        done = [
            conv_norm(rows[r - 1], rows[r], rows[r + 1], conv, gain)
            for r in range(1, row_count - 1)
        ]
        results.append([jnp.concatenate(part, axis=0) for part in zip(*done)])
    put_rows(first, results, mixed, normed, rolled)


def edge_kernel(first, emb, before, after, conv_ref, gain_ref, mixed, normed, rolled):
    row_count = emb.shape[1]
    conv = conv_ref[...]
    gain = gain_ref[...]
    results = []
    for k in range(2):
        done = [
            conv_norm(before[k], emb[k, 0], emb[k, 1], conv, gain),
            conv_norm(emb[k, row_count - 2], emb[k, row_count - 1], after[k], conv, gain),
        ]
        results.append([jnp.concatenate(part, axis=0) for part in zip(*done)])
    put_rows(first, results, mixed, normed, rolled)


def attend_kernel(
    tm_ref, x_lo, x_hi, own_lo, own_hi, lo, hi, anchors, m_lo, m_hi, wq_t, wk, wv_t, w_out, *rest
):
    out, mask = rest[-2:]
    tm = tm_ref[0]
    width = x_lo.shape[-1]
    queries = WINDOW * GROUP
    lanes = 2 * queries
    slabs = 2 * WINDOW + ANCHORS

    @pl.when(pl.program_id(0) == 0)
    def _():
        row = lax.broadcasted_iota(jnp.int32, (slabs * GROUP, lanes), 0)
        lane = lax.broadcasted_iota(jnp.int32, (slabs * GROUP, lanes), 1)
        u = row // GROUP
        t = (lane % queries) // GROUP
        met = (row - lane + lanes) % GROUP
        mine = (u < WINDOW) & (u % GROUP == met) & (u <= t)
        past = (u >= WINDOW) & (u < 2 * WINDOW) & (u % GROUP == met) & (u - WINDOW > t)
        first = (u >= 2 * WINDOW) & (u - 2 * WINDOW == met)
        mask[...] = jnp.where(mine | past | first, 1.0, 0.0).astype(BF16)

    sub = lax.broadcasted_iota(jnp.int32, (GROUP, lanes), 0)
    lane = lax.broadcasted_iota(jnp.int32, (GROUP, lanes), 1)
    t = (lane % queries) // GROUP
    met = (sub - lane + lanes) % GROUP
    places = []
    for b in range(WINDOW // GROUP):
        u = met + b * GROUP
        places.append(jnp.where(u <= t, u, u + WINDOW))
    open_window = [(c < WINDOW) | (tm > 0) for c in places]
    open_anchor = (met < ANCHORS) & (met < tm * WINDOW + t - (WINDOW - 1))

    anchor_rows = ANCHORS * GROUP
    window_rows = 2 * queries
    x = jnp.concatenate([ref[i] for i in range(STEP) for ref in (x_lo, x_hi)], axis=0)
    window = [ref[i] for i in range(STEP) for ref in (own_lo, own_hi, lo, hi)]
    window = jnp.concatenate(window, axis=0)
    first = anchors[...].reshape(STEP * anchor_rows, width)
    q_t = lax.dot_general(wq_t[...], x, NT, preferred_element_type=F32).astype(BF16)
    q_t = (q_t * 0.125).astype(BF16)
    k_all = jnp.dot(
        jnp.concatenate([window, first], axis=0), wk[...], preferred_element_type=F32
    ).astype(BF16)
    v_all = lax.dot_general(wv_t[...], window, NT, preferred_element_type=F32).astype(BF16)
    va_t = lax.dot_general(wv_t[...], first, NT, preferred_element_type=F32).astype(BF16)
    blank = jnp.zeros((64, queries), BF16)
    no_rows = jnp.zeros((anchor_rows, lanes), BF16)
    columns = []
    for i in range(STEP):
        at = STEP * window_rows + i * anchor_rows
        k = jnp.concatenate(
            [k_all[i * window_rows : (i + 1) * window_rows], k_all[at : at + anchor_rows]], axis=0
        )
        v_t = v_all[:, i * window_rows : (i + 1) * window_rows]
        parts = []
        for pair in range(width // 128):
            at = pair * 128
            across = slice(i * queries, (i + 1) * queries)
            left = jnp.concatenate([q_t[at : at + 64, across], blank], axis=0)
            right = jnp.concatenate([blank, q_t[at + 64 : at + 128, across]], axis=0)
            s = jnp.dot(
                k[:, at : at + 128],
                jnp.concatenate([left, right], axis=1),
                preferred_element_type=F32,
            )
            s = [s[j * GROUP : (j + 1) * GROUP] for j in range(slabs)]
            merged = []
            for b in range(WINDOW // GROUP):
                w = s[b * GROUP]
                for d in range(GROUP):
                    u = b * GROUP + d
                    if d > 0:
                        w = jnp.where(places[b] == u, s[u], w)
                    w = jnp.where(places[b] == WINDOW + u, s[WINDOW + u], w)
                merged.append(jnp.where(open_window[b], w, -1e30))
            w = s[2 * WINDOW]
            for u in range(1, ANCHORS):
                w = jnp.where(met == u, s[2 * WINDOW + u], w)
            merged.append(jnp.where(open_anchor, w, -1e30))
            top = jnp.max(
                jnp.maximum(jnp.maximum(merged[0], merged[1]), merged[2]), axis=0, keepdims=True
            )
            e = [jnp.exp(w - top) for w in merged]
            total = jnp.sum(e[0] + e[1] + e[2], axis=0, keepdims=True)
            over = 1.0 / total
            p = [w * over for w in e]
            p = [jnp.concatenate([w, w], axis=0).astype(BF16) for w in p]
            spread = []
            for j in range(slabs // 2):
                b = (2 * j % WINDOW) // GROUP if j < WINDOW else 2
                spread.append(p[b] * mask[j * 16 : (j + 1) * 16, :])
            p_window = jnp.concatenate(spread[:WINDOW], axis=0)
            p_first = jnp.concatenate(spread[WINDOW:], axis=0)
            p_first = [p_first if n == i else no_rows for n in range(STEP)]
            o = jnp.dot(v_t[at : at + 128], p_window, preferred_element_type=F32)
            o += jnp.dot(
                va_t[at : at + 128],
                jnp.concatenate(p_first, axis=0),
                preferred_element_type=F32,
            )
            parts += [o[:64, :queries], o[64:, queries:]]
        columns.append(jnp.concatenate(parts, axis=0).astype(BF16))
    attended = jnp.concatenate(columns, axis=1)
    result = lax.dot_general(attended, w_out[...], TN, preferred_element_type=F32)
    results = []
    for i in range(STEP):
        mixed = jnp.concatenate([m_lo[i], m_hi[i]], axis=0)
        total = result[i * queries : (i + 1) * queries] + mixed
        results.append(total.reshape(WINDOW, GROUP, width))
    out[...] = jnp.concatenate(results, axis=1).astype(BF16).reshape(out.shape)


def params():
    return pltpu.CompilerParams(vmem_limit_bytes=VMEM_LIMIT)


def small():
    return pl.CostEstimate(flops=1000, bytes_accessed=1000, transcendentals=0)


def whole(a):
    return pl.BlockSpec(a.shape, lambda f: (0,) * a.ndim)


def row_outputs(count, positions, width):
    groups = positions // GROUP
    spec = pl.BlockSpec((groups, 2 * GROUP, width), lambda f: (0, f, 0))
    shapes = [
        jax.ShapeDtypeStruct((groups, count * GROUP, width), dtype) for dtype in (F32, BF16, BF16)
    ]
    return [spec] * 3, shapes


def embed(first, count, ids, frames, actions, table, conv, gain):
    _, row_count, cols, width = frames.shape
    strip = jax.ShapeDtypeStruct((count, cols, width), BF16)
    strip_spec = pl.BlockSpec((2, cols, width), lambda f: (f, 0, 0))
    block = (2, row_count, cols, width)
    skip = first // 2
    specs, shapes = row_outputs(count, (row_count - 2) * cols, width)
    return pl.pallas_call(
        functools.partial(embed_kernel, first),
        grid=(count // 2,),
        in_specs=[
            pl.BlockSpec((1, 1, 2 * row_count * cols), lambda f: (f + skip, 0, 0)),
            pl.BlockSpec(block, lambda f: (f + skip, 0, 0, 0)),
            whole(actions),
            whole(table),
            whole(conv),
            whole(gain),
        ],
        out_specs=[pl.BlockSpec(block, lambda f: (f, 0, 0, 0)), strip_spec, strip_spec] + specs,
        out_shape=[
            jax.ShapeDtypeStruct((count, row_count, cols, width), BF16),
            strip,
            strip,
        ]
        + shapes,
        compiler_params=params(),
        cost_estimate=small(),
        name="embed",
    )(ids, frames, actions, table, conv, gain)


def edge(first, emb, before, after, conv, gain):
    count, row_count, cols, width = emb.shape
    strip_spec = pl.BlockSpec((2, cols, width), lambda f: (f, 0, 0))
    frame_spec = pl.BlockSpec((2, row_count, cols, width), lambda f: (f, 0, 0, 0))
    specs, shapes = row_outputs(count, 2 * cols, width)
    return pl.pallas_call(
        functools.partial(edge_kernel, first),
        grid=(count // 2,),
        in_specs=[frame_spec, strip_spec, strip_spec, whole(conv), whole(gain)],
        out_specs=specs,
        out_shape=shapes,
        compiler_params=params(),
        cost_estimate=small(),
        name="edge",
    )(emb, before, after, conv, gain)


def attend(tm, blocks, weights, out, shape, positions, row_of):
    count, _, cols, width = shape
    per_row = cols // (STEP * GROUP)

    def block(a, start):
        return pl.BlockSpec((STEP,) + a.shape[1:], lambda g: (g + start // STEP, 0, 0))

    args = [tm, *[a for a, _ in blocks], *weights]
    specs = [pl.BlockSpec(memory_space=pltpu.SMEM)]
    specs += [block(a, start) for a, start in blocks] + [whole(w) for w in weights]
    aliases = {}
    if out is not None:
        aliases = {len(args): 0}
        args.append(out)
        specs.append(pl.BlockSpec(memory_space=pl.ANY))
    return pl.pallas_call(
        attend_kernel,
        grid=(positions // (STEP * GROUP),),
        in_specs=specs,
        out_specs=pl.BlockSpec(
            (count, 1, STEP * GROUP, width),
            lambda g: (0, row_of(g // per_row), g % per_row, 0),
        ),
        out_shape=jax.ShapeDtypeStruct(shape, BF16),
        scratch_shapes=[
            pltpu.VMEM(((2 * WINDOW + ANCHORS) * GROUP, 2 * WINDOW * GROUP), BF16)
        ],
        input_output_aliases=aliases,
        compiler_params=params(),
        cost_estimate=small(),
        name="attend",
    )(*args)


def send(x, by):
    count = lax.axis_size("tm")
    return lax.ppermute(x, "tm", [(i, i + by) for i in range(count - by)])


def anchors_of(first, lo, tm):
    count = lax.axis_size("tm")
    anchors = jnp.where(tm == 0, first, lo)
    by = count // 2
    while by >= 2:
        pairs = [(i, i + by) for i in range(count - by) if i % (2 * by) < 2]
        got = lax.ppermute(anchors, "tm", pairs)
        place = tm % (2 * by)
        anchors = jnp.where((place == by) | (place == by + 1), got, anchors)
        by //= 2
    return anchors


def halo(top, bottom):
    strips = lax.axis_size("space")
    up = [(i, i + 1) for i in range(strips - 1)]
    return lax.ppermute(bottom, "space", up), lax.ppermute(top, "space", [(j, i) for i, j in up])


def on_device(
    frames,
    token_ids,
    action_ids,
    token_table,
    action_table,
    conv_weight,
    norm_gain,
    w_query,
    w_key,
    w_value,
    w_out,
):
    shape = frames.shape
    width = shape[3]
    tm = lax.axis_index("tm")
    tm_arg = tm.astype(jnp.int32).reshape(1)
    ids = token_ids.reshape(shape[0] // 2, 1, -1)
    onehot = (action_ids[:, None] == jnp.arange(ACTIONS, dtype=jnp.int32)[None, :]).astype(BF16)
    actions = jnp.dot(onehot, action_table, preferred_element_type=F32)
    conv = conv_weight.reshape(9, width).astype(F32)
    gain = norm_gain.reshape(1, width).astype(F32)
    weights = [w_query.T, w_key, w_value.T, w_out]

    cols = shape[2]
    inner = (shape[1] - 2) * cols // GROUP
    row = cols // GROUP
    shared = (ids, frames, actions, token_table, conv, gain)

    emb, top, bottom, mixed_a, normed_a, rolled_a = embed(0, ANCHORS, *shared)
    mixed_b, normed_b, rolled_b = edge(0, emb, *halo(top, bottom), conv, gain)
    first = jnp.concatenate([rolled_a, rolled_b], axis=0)
    lo = send(first, 1)
    emb, top, bottom, mixed_c, normed_c, rolled_c = embed(ANCHORS, shape[0] - ANCHORS, *shared)
    lo, _ = lax.optimization_barrier((lo, rolled_c))
    anchors = anchors_of(first, lo, tm)
    hi = send(rolled_c, 1)
    mixed_d, normed_d, rolled_d = edge(ANCHORS, emb, *halo(top, bottom), conv, gain)

    def blocks(x_lo, x_hi, own_hi, hi, m_lo, m_hi, start, at, hi_at):
        return [
            (x_lo, at),
            (x_hi, at),
            (first, start + at),
            (own_hi, at),
            (lo, start + at),
            (hi, hi_at),
            (anchors, start + at),
            (m_lo, at),
            (m_hi, at),
        ]

    out = attend(
        tm_arg,
        blocks(normed_a, normed_c, rolled_c, hi, mixed_a, mixed_c, 0, 0, 0),
        weights,
        None,
        shape,
        inner * GROUP,
        lambda r: r + 1,
    )
    to_send, _ = lax.optimization_barrier((rolled_d, hi))
    later = [send(to_send[r * row : (r + 1) * row], 1) for r in range(2)]
    for r in range(2):
        out = attend(
            tm_arg,
            blocks(normed_b, normed_d, rolled_d, later[r], mixed_b, mixed_d, inner, r * row, 0),
            weights,
            out,
            shape,
            cols,
            lambda _, r=r: r * (shape[1] - 1),
        )
    return out


def solution(mesh):
    in_specs = (
        P("tm", "space", None, None),
        P(None, "tm", "space", None),
        P("tm"),
        P(),
        P(),
        P(),
        P(),
        P(),
        P(),
        P(),
        P(),
    )
    out_specs = P("tm", "space", None, None)
    return jax.shard_map(
        on_device, mesh=mesh, in_specs=in_specs, out_specs=out_specs, check_vma=False
    )
```

```python
import functools

import jax
import jax.numpy as jnp
from jax import lax
from jax.experimental import pallas as pl
from jax.experimental.pallas import tpu as pltpu
from jax.sharding import PartitionSpec as P

HEADS = 6
ACTIONS = 8
WINDOW = 16
ANCHORS = 4
GROUP = 8
STEP = 4
F32 = jnp.float32
BF16 = jnp.bfloat16
NT = (((1,), (1,)), ((), ()))
TN = (((0,), (0,)), ((), ()))
VMEM_LIMIT = 48 * 1024 * 1024


def shift_cols(y, by):
    cols = y.shape[0]
    rolled = pltpu.roll(y, by % cols, 0)
    at = lax.broadcasted_iota(jnp.int32, y.shape, 0)
    edge = 0 if by == 1 else cols - 1
    return jnp.where(at == edge, 0.0, rolled)


def conv_norm(above, here, below, conv, gain):
    rows = [r.astype(F32) for r in (above, here, below)]
    sums = []
    for j in range(3):
        sums.append(
            rows[0] * conv[j : j + 1]
            + rows[1] * conv[3 + j : 4 + j]
            + rows[2] * conv[6 + j : 7 + j]
        )
    mixed = rows[1] + sums[1] + shift_cols(sums[0], 1) + shift_cols(sums[2], -1)
    scale = lax.rsqrt(jnp.mean(mixed * mixed, axis=-1, keepdims=True) + 1e-06)
    return mixed, mixed * scale * gain


def grouped(first, second):
    width = first.shape[-1]
    first = first.reshape(-1, GROUP, width)
    second = second.reshape(-1, GROUP, width)
    return jnp.concatenate([first, second], axis=1)


def put_rows(first, results, mixed, normed, rolled):
    frame = pl.program_id(0) * 2 + first
    turned = []
    for k in range(2):
        n = results[k][1].reshape(-1, GROUP, results[k][1].shape[-1])
        turned.append(pltpu.roll(n, lax.rem(frame + k, GROUP), 1))
    mixed[...] = grouped(results[0][0], results[1][0])
    normed[...] = grouped(results[0][1], results[1][1]).astype(BF16)
    rolled[...] = jnp.concatenate(turned, axis=1).astype(BF16)


def embed_kernel(
    first, ids, frames, actions, table, conv_ref, gain_ref, emb, top, bottom, mixed, normed, rolled
):
    frame = pl.program_id(0) * 2 + first
    row_count, cols, width = frames.shape[1:]
    vocab = table.shape[0]
    count = 2 * row_count * cols
    row_ids = ids[0].astype(F32)
    codes = jnp.transpose(jnp.broadcast_to(row_ids, (128, count)), (1, 0))
    lane = lax.broadcasted_iota(jnp.int32, (count, 128), 1).astype(F32)
    onehot = [
        jnp.where(codes == lane + 128.0 * k, 1.0, 0.0).astype(BF16) for k in range(vocab // 128)
    ]
    tokens = jnp.dot(jnp.concatenate(onehot, axis=1), table[...], preferred_element_type=F32)
    conv = conv_ref[...]
    gain = gain_ref[...]
    results = []
    for k in range(2):
        action = actions[pl.ds(frame + k, 1), :]
        rows = []
        for r in range(row_count):
            at = (k * row_count + r) * cols
            row = frames[k, r].astype(F32) + tokens[at : at + cols] + action
            row = row.astype(BF16)
            emb[k, r] = row
            rows.append(row)
        top[k] = rows[0]
        bottom[k] = rows[-1]
        done = [
            conv_norm(rows[r - 1], rows[r], rows[r + 1], conv, gain)
            for r in range(1, row_count - 1)
        ]
        results.append([jnp.concatenate(part, axis=0) for part in zip(*done)])
    put_rows(first, results, mixed, normed, rolled)


def edge_kernel(first, emb, before, after, conv_ref, gain_ref, mixed, normed, rolled):
    row_count = emb.shape[1]
    conv = conv_ref[...]
    gain = gain_ref[...]
    results = []
    for k in range(2):
        done = [
            conv_norm(before[k], emb[k, 0], emb[k, 1], conv, gain),
            conv_norm(emb[k, row_count - 2], emb[k, row_count - 1], after[k], conv, gain),
        ]
        results.append([jnp.concatenate(part, axis=0) for part in zip(*done)])
    put_rows(first, results, mixed, normed, rolled)


def attend_kernel(
    tm_ref, x_lo, x_hi, own_lo, own_hi, lo, hi, anchors, m_lo, m_hi, wq_t, wk, wv_t, w_out, *rest
):
    out, mask, scores, spread, spread_first = rest[-5:]
    tm = tm_ref[0]
    width = x_lo.shape[-1]
    queries = WINDOW * GROUP
    pairs = width // 128
    columns = STEP * pairs * 2
    slabs = 2 * WINDOW + ANCHORS
    anchor_rows = ANCHORS * GROUP
    window_rows = 2 * queries

    @pl.when(pl.program_id(0) == 0)
    def _():
        row = lax.broadcasted_iota(jnp.int32, (slabs * GROUP, queries), 0)
        lane = lax.broadcasted_iota(jnp.int32, (slabs * GROUP, queries), 1)
        u = row // GROUP
        t = lane // GROUP
        met = (row - lane + queries) % GROUP
        mine = (u < WINDOW) & (u % GROUP == met) & (u <= t)
        past = (u >= WINDOW) & (u < 2 * WINDOW) & (u % GROUP == met) & (u - WINDOW > t)
        first = (u >= 2 * WINDOW) & (u - 2 * WINDOW == met)
        mask[...] = jnp.where(mine | past | first, 1.0, 0.0).astype(BF16)
        spread_first[...] = jnp.zeros(spread_first.shape, BF16)

    x = jnp.concatenate([ref[i] for i in range(STEP) for ref in (x_lo, x_hi)], axis=0)
    window = [ref[i] for i in range(STEP) for ref in (own_lo, own_hi, lo, hi)]
    window = jnp.concatenate(window, axis=0)
    first = anchors[...].reshape(STEP * anchor_rows, width)
    q_t = lax.dot_general(wq_t[...], x, NT, preferred_element_type=F32).astype(BF16)
    q_t = (q_t * 0.125).astype(BF16)
    k_all = jnp.dot(
        jnp.concatenate([window, first], axis=0), wk[...], preferred_element_type=F32
    ).astype(BF16)
    v_t = lax.dot_general(wv_t[...], window, NT, preferred_element_type=F32).astype(BF16)
    va_t = lax.dot_general(wv_t[...], first, NT, preferred_element_type=F32).astype(BF16)

    blank = jnp.zeros((64, queries), BF16)
    for i in range(STEP):
        at = STEP * window_rows + i * anchor_rows
        k = jnp.concatenate(
            [k_all[i * window_rows : (i + 1) * window_rows], k_all[at : at + anchor_rows]], axis=0
        )
        for pair in range(pairs):
            at = pair * 128
            across = slice(i * queries, (i + 1) * queries)
            left = jnp.concatenate([q_t[at : at + 64, across], blank], axis=0)
            right = jnp.concatenate([blank, q_t[at + 64 : at + 128, across]], axis=0)
            column = (i * pairs + pair) * 2 * queries
            scores[:, column : column + 2 * queries] = jnp.dot(
                k[:, at : at + 128],
                jnp.concatenate([left, right], axis=1),
                preferred_element_type=F32,
            )

    sub = lax.broadcasted_iota(jnp.int32, (GROUP, queries), 0)
    lane = lax.broadcasted_iota(jnp.int32, (GROUP, queries), 1)
    t = lane // GROUP
    met = (sub - lane + queries) % GROUP

    def slab(u, c):
        return scores[u * GROUP : (u + 1) * GROUP, c * queries : (c + 1) * queries]

    merged = []
    for b in range(WINDOW // GROUP):
        u = met + b * GROUP
        place = jnp.where(u <= t, u, u + WINDOW)
        w = [slab(b * GROUP, c) for c in range(columns)]
        for d in range(GROUP):
            for u in (b * GROUP + d, WINDOW + b * GROUP + d):
                if u != b * GROUP:
                    here = place == u
                    w = [jnp.where(here, slab(u, c), w[c]) for c in range(columns)]
        seen = (place < WINDOW) | (tm > 0)
        merged.append([jnp.where(seen, v, -1e30) for v in w])
    w = [slab(2 * WINDOW, c) for c in range(columns)]
    for u in range(1, ANCHORS):
        here = met == u
        w = [jnp.where(here, slab(2 * WINDOW + u, c), w[c]) for c in range(columns)]
    seen = (met < ANCHORS) & (met < tm * WINDOW + t - (WINDOW - 1))
    merged.append([jnp.where(seen, v, -1e30) for v in w])

    merged = [jnp.concatenate(w, axis=1) for w in merged]
    top = jnp.max(
        jnp.maximum(jnp.maximum(merged[0], merged[1]), merged[2]), axis=0, keepdims=True
    )
    e = [jnp.exp(w - top) for w in merged]
    over = 1.0 / jnp.sum(e[0] + e[1] + e[2], axis=0, keepdims=True)
    probs = [w * over for w in e]
    probs = [jnp.concatenate([w, w], axis=0).astype(BF16) for w in probs]

    for j in range(slabs // 2):
        b = (2 * j % WINDOW) // GROUP if j < WINDOW else 2
        here = mask[j * 16 : (j + 1) * 16, :]
        for c in range(columns):
            piece = probs[b][:, c * queries : (c + 1) * queries] * here
            across = slice(c * queries, (c + 1) * queries)
            if j < WINDOW:
                spread[j * 16 : (j + 1) * 16, across] = piece
            else:
                at = c // (2 * pairs) * anchor_rows + (j - WINDOW) * 16
                spread_first[at : at + 16, across] = piece

    attended = []
    for i in range(STEP):
        parts = []
        for pair in range(pairs):
            at = slice(pair * 128, (pair + 1) * 128)
            column = (i * pairs + pair) * 2 * queries
            across = slice(column, column + 2 * queries)
            o = jnp.dot(
                v_t[at, i * window_rows : (i + 1) * window_rows],
                spread[:, across],
                preferred_element_type=F32,
            )
            o += jnp.dot(va_t[at], spread_first[:, across], preferred_element_type=F32)
            parts += [o[:64, :queries], o[64:, queries:]]
        attended.append(jnp.concatenate(parts, axis=0).astype(BF16))
    attended = jnp.concatenate(attended, axis=1)
    result = lax.dot_general(attended, w_out[...], TN, preferred_element_type=F32)
    results = []
    for i in range(STEP):
        mixed = jnp.concatenate([m_lo[i], m_hi[i]], axis=0)
        total = result[i * queries : (i + 1) * queries] + mixed
        results.append(total.reshape(WINDOW, GROUP, width))
    out[...] = jnp.concatenate(results, axis=1).astype(BF16).reshape(out.shape)


def params():
    return pltpu.CompilerParams(vmem_limit_bytes=VMEM_LIMIT)


def small():
    return pl.CostEstimate(flops=1000, bytes_accessed=1000, transcendentals=0)


def whole(a):
    return pl.BlockSpec(a.shape, lambda f: (0,) * a.ndim)


def row_outputs(count, positions, width):
    groups = positions // GROUP
    spec = pl.BlockSpec((groups, 2 * GROUP, width), lambda f: (0, f, 0))
    shapes = [
        jax.ShapeDtypeStruct((groups, count * GROUP, width), dtype) for dtype in (F32, BF16, BF16)
    ]
    return [spec] * 3, shapes


def embed(first, count, ids, frames, actions, table, conv, gain):
    _, row_count, cols, width = frames.shape
    strip = jax.ShapeDtypeStruct((count, cols, width), BF16)
    strip_spec = pl.BlockSpec((2, cols, width), lambda f: (f, 0, 0))
    block = (2, row_count, cols, width)
    skip = first // 2
    specs, shapes = row_outputs(count, (row_count - 2) * cols, width)
    return pl.pallas_call(
        functools.partial(embed_kernel, first),
        grid=(count // 2,),
        in_specs=[
            pl.BlockSpec((1, 1, 2 * row_count * cols), lambda f: (f + skip, 0, 0)),
            pl.BlockSpec(block, lambda f: (f + skip, 0, 0, 0)),
            whole(actions),
            whole(table),
            whole(conv),
            whole(gain),
        ],
        out_specs=[pl.BlockSpec(block, lambda f: (f, 0, 0, 0)), strip_spec, strip_spec] + specs,
        out_shape=[
            jax.ShapeDtypeStruct((count, row_count, cols, width), BF16),
            strip,
            strip,
        ]
        + shapes,
        compiler_params=params(),
        cost_estimate=small(),
        name="embed",
    )(ids, frames, actions, table, conv, gain)


def edge(first, emb, before, after, conv, gain):
    count, row_count, cols, width = emb.shape
    strip_spec = pl.BlockSpec((2, cols, width), lambda f: (f, 0, 0))
    frame_spec = pl.BlockSpec((2, row_count, cols, width), lambda f: (f, 0, 0, 0))
    specs, shapes = row_outputs(count, 2 * cols, width)
    return pl.pallas_call(
        functools.partial(edge_kernel, first),
        grid=(count // 2,),
        in_specs=[frame_spec, strip_spec, strip_spec, whole(conv), whole(gain)],
        out_specs=specs,
        out_shape=shapes,
        compiler_params=params(),
        cost_estimate=small(),
        name="edge",
    )(emb, before, after, conv, gain)


def attend(tm, blocks, weights, out, shape, positions, row_of):
    count, _, cols, width = shape
    per_row = cols // (STEP * GROUP)
    keys = (2 * WINDOW + ANCHORS) * GROUP
    lanes = STEP * (width // 64) * WINDOW * GROUP

    def block(a, start):
        return pl.BlockSpec((STEP,) + a.shape[1:], lambda g: (g + start // STEP, 0, 0))

    args = [tm, *[a for a, _ in blocks], *weights]
    specs = [pl.BlockSpec(memory_space=pltpu.SMEM)]
    specs += [block(a, start) for a, start in blocks] + [whole(w) for w in weights]
    aliases = {}
    if out is not None:
        aliases = {len(args): 0}
        args.append(out)
        specs.append(pl.BlockSpec(memory_space=pl.ANY))
    return pl.pallas_call(
        attend_kernel,
        grid=(positions // (STEP * GROUP),),
        in_specs=specs,
        out_specs=pl.BlockSpec(
            (count, 1, STEP * GROUP, width),
            lambda g: (0, row_of(g // per_row), g % per_row, 0),
        ),
        out_shape=jax.ShapeDtypeStruct(shape, BF16),
        scratch_shapes=[
            pltpu.VMEM((keys, WINDOW * GROUP), BF16),
            pltpu.VMEM((keys, lanes), F32),
            pltpu.VMEM((2 * WINDOW * GROUP, lanes), BF16),
            pltpu.VMEM((STEP * ANCHORS * GROUP, lanes), BF16),
        ],
        input_output_aliases=aliases,
        compiler_params=params(),
        cost_estimate=small(),
        name="attend",
    )(*args)


def send(x, by):
    count = lax.axis_size("tm")
    return lax.ppermute(x, "tm", [(i, i + by) for i in range(count - by)])


def anchors_of(first, lo, tm):
    count = lax.axis_size("tm")
    anchors = jnp.where(tm == 0, first, lo)
    by = count // 2
    while by >= 2:
        pairs = [(i, i + by) for i in range(count - by) if i % (2 * by) < 2]
        got = lax.ppermute(anchors, "tm", pairs)
        place = tm % (2 * by)
        anchors = jnp.where((place == by) | (place == by + 1), got, anchors)
        by //= 2
    return anchors


def halo(top, bottom):
    strips = lax.axis_size("space")
    up = [(i, i + 1) for i in range(strips - 1)]
    return lax.ppermute(bottom, "space", up), lax.ppermute(top, "space", [(j, i) for i, j in up])


def on_device(
    frames,
    token_ids,
    action_ids,
    token_table,
    action_table,
    conv_weight,
    norm_gain,
    w_query,
    w_key,
    w_value,
    w_out,
):
    shape = frames.shape
    width = shape[3]
    tm = lax.axis_index("tm")
    tm_arg = tm.astype(jnp.int32).reshape(1)
    ids = token_ids.reshape(shape[0] // 2, 1, -1)
    onehot = (action_ids[:, None] == jnp.arange(ACTIONS, dtype=jnp.int32)[None, :]).astype(BF16)
    actions = jnp.dot(onehot, action_table, preferred_element_type=F32)
    conv = conv_weight.reshape(9, width).astype(F32)
    gain = norm_gain.reshape(1, width).astype(F32)
    weights = [w_query.T, w_key, w_value.T, w_out]

    cols = shape[2]
    inner = (shape[1] - 2) * cols // GROUP
    row = cols // GROUP
    shared = (ids, frames, actions, token_table, conv, gain)

    emb, top, bottom, mixed_a, normed_a, rolled_a = embed(0, ANCHORS, *shared)
    mixed_b, normed_b, rolled_b = edge(0, emb, *halo(top, bottom), conv, gain)
    first = jnp.concatenate([rolled_a, rolled_b], axis=0)
    lo = send(first, 1)
    emb, top, bottom, mixed_c, normed_c, rolled_c = embed(ANCHORS, shape[0] - ANCHORS, *shared)
    lo, _ = lax.optimization_barrier((lo, rolled_c))
    anchors = anchors_of(first, lo, tm)
    hi = [send(rolled_c[r * row : (r + 1) * row], 1) for r in range(inner // row)]
    mixed_d, normed_d, rolled_d = edge(ANCHORS, emb, *halo(top, bottom), conv, gain)

    def blocks(x_lo, x_hi, own_hi, hi, m_lo, m_hi, start, at, hi_at):
        return [
            (x_lo, at),
            (x_hi, at),
            (first, start + at),
            (own_hi, at),
            (lo, start + at),
            (hi, hi_at),
            (anchors, start + at),
            (m_lo, at),
            (m_hi, at),
        ]

    out = None
    for r in range(inner // row):
        out = attend(
            tm_arg,
            blocks(normed_a, normed_c, rolled_c, hi[r], mixed_a, mixed_c, 0, r * row, 0),
            weights,
            out,
            shape,
            cols,
            lambda _, r=r: r + 1,
        )
    to_send, _ = lax.optimization_barrier((rolled_d, hi[0]))
    later = [send(to_send[r * row : (r + 1) * row], 1) for r in range(2)]
    for r in range(2):
        out = attend(
            tm_arg,
            blocks(normed_b, normed_d, rolled_d, later[r], mixed_b, mixed_d, inner, r * row, 0),
            weights,
            out,
            shape,
            cols,
            lambda _, r=r: r * (shape[1] - 1),
        )
    return out


def solution(mesh):
    in_specs = (
        P("tm", "space", None, None),
        P(None, "tm", "space", None),
        P("tm"),
        P(),
        P(),
        P(),
        P(),
        P(),
        P(),
        P(),
        P(),
    )
    out_specs = P("tm", "space", None, None)
    return jax.shard_map(
        on_device, mesh=mesh, in_specs=in_specs, out_specs=out_specs, check_vma=False
    )
```

```python
import functools

import jax
import jax.numpy as jnp
from jax import lax
from jax.experimental import pallas as pl
from jax.experimental.pallas import tpu as pltpu
from jax.sharding import PartitionSpec as P

HEADS = 6
ACTIONS = 8
WINDOW = 16
ANCHORS = 4
GROUP = 8
STEP = 4
F32 = jnp.float32
BF16 = jnp.bfloat16
NT = (((1,), (1,)), ((), ()))
TN = (((0,), (0,)), ((), ()))
VMEM_LIMIT = 48 * 1024 * 1024


def shift_cols(y, by):
    cols = y.shape[0]
    rolled = pltpu.roll(y, by % cols, 0)
    at = lax.broadcasted_iota(jnp.int32, y.shape, 0)
    edge = 0 if by == 1 else cols - 1
    return jnp.where(at == edge, 0.0, rolled)


def conv_norm(above, here, below, conv, gain):
    rows = [r.astype(F32) for r in (above, here, below)]
    sums = []
    for j in range(3):
        sums.append(
            rows[0] * conv[j : j + 1]
            + rows[1] * conv[3 + j : 4 + j]
            + rows[2] * conv[6 + j : 7 + j]
        )
    mixed = rows[1] + sums[1] + shift_cols(sums[0], 1) + shift_cols(sums[2], -1)
    scale = lax.rsqrt(jnp.mean(mixed * mixed, axis=-1, keepdims=True) + 1e-06)
    return mixed, mixed * scale * gain


def grouped(first, second):
    width = first.shape[-1]
    first = first.reshape(-1, GROUP, width)
    second = second.reshape(-1, GROUP, width)
    return jnp.concatenate([first, second], axis=1)


def put_rows(first, results, mixed, normed, rolled):
    frame = pl.program_id(0) * 2 + first
    turned = []
    for k in range(2):
        n = results[k][1].reshape(-1, GROUP, results[k][1].shape[-1])
        turned.append(pltpu.roll(n, lax.rem(frame + k, GROUP), 1))
    mixed[...] = grouped(results[0][0], results[1][0])
    normed[...] = grouped(results[0][1], results[1][1]).astype(BF16)
    rolled[...] = jnp.concatenate(turned, axis=1).astype(BF16)


def embed_kernel(
    first, ids, frames, actions, table, conv_ref, gain_ref, emb, top, bottom, mixed, normed, rolled
):
    frame = pl.program_id(0) * 2 + first
    row_count, cols, width = frames.shape[1:]
    vocab = table.shape[0]
    count = 2 * row_count * cols
    row_ids = ids[0].astype(F32)
    codes = jnp.transpose(jnp.broadcast_to(row_ids, (128, count)), (1, 0))
    lane = lax.broadcasted_iota(jnp.int32, (count, 128), 1).astype(F32)
    onehot = [
        jnp.where(codes == lane + 128.0 * k, 1.0, 0.0).astype(BF16) for k in range(vocab // 128)
    ]
    tokens = jnp.dot(jnp.concatenate(onehot, axis=1), table[...], preferred_element_type=F32)
    conv = conv_ref[...]
    gain = gain_ref[...]
    results = []
    for k in range(2):
        action = actions[pl.ds(frame + k, 1), :]
        rows = []
        for r in range(row_count):
            at = (k * row_count + r) * cols
            row = frames[k, r].astype(F32) + tokens[at : at + cols] + action
            row = row.astype(BF16)
            emb[k, r] = row
            rows.append(row)
        top[k] = rows[0]
        bottom[k] = rows[-1]
        done = [
            conv_norm(rows[r - 1], rows[r], rows[r + 1], conv, gain)
            for r in range(1, row_count - 1)
        ]
        results.append([jnp.concatenate(part, axis=0) for part in zip(*done)])
    put_rows(first, results, mixed, normed, rolled)


def edge_kernel(first, emb, before, after, conv_ref, gain_ref, mixed, normed, rolled):
    row_count = emb.shape[1]
    conv = conv_ref[...]
    gain = gain_ref[...]
    results = []
    for k in range(2):
        done = [
            conv_norm(before[k], emb[k, 0], emb[k, 1], conv, gain),
            conv_norm(emb[k, row_count - 2], emb[k, row_count - 1], after[k], conv, gain),
        ]
        results.append([jnp.concatenate(part, axis=0) for part in zip(*done)])
    put_rows(first, results, mixed, normed, rolled)


def attend_kernel(
    tm_ref, x_lo, x_hi, own_lo, own_hi, lo, hi, anchors, m_lo, m_hi, wq_t, wk, wv_t, w_out, *rest
):
    out, mask, scores, spread, spread_first = rest[-5:]
    tm = tm_ref[0]
    width = x_lo.shape[-1]
    queries = WINDOW * GROUP
    pairs = width // 128
    columns = STEP * pairs * 2
    slabs = 2 * WINDOW + ANCHORS
    anchor_rows = ANCHORS * GROUP
    window_rows = 2 * queries

    @pl.when(pl.program_id(0) == 0)
    def _():
        row = lax.broadcasted_iota(jnp.int32, (slabs * GROUP, queries), 0)
        lane = lax.broadcasted_iota(jnp.int32, (slabs * GROUP, queries), 1)
        u = row // GROUP
        t = lane // GROUP
        met = (row - lane + queries) % GROUP
        mine = (u < WINDOW) & (u % GROUP == met) & (u <= t)
        past = (u >= WINDOW) & (u < 2 * WINDOW) & (u % GROUP == met) & (u - WINDOW > t)
        first = (u >= 2 * WINDOW) & (u - 2 * WINDOW == met)
        mask[...] = jnp.where(mine | past | first, 1.0, 0.0).astype(BF16)
        spread_first[...] = jnp.zeros(spread_first.shape, BF16)

    x = jnp.concatenate([ref[i] for i in range(STEP) for ref in (x_lo, x_hi)], axis=0)
    window = [ref[i] for i in range(STEP) for ref in (own_lo, own_hi, lo, hi)]
    window = jnp.concatenate(window, axis=0)
    first = anchors[...].reshape(STEP * anchor_rows, width)
    q_t = lax.dot_general(wq_t[...], x, NT, preferred_element_type=F32).astype(BF16)
    q_t = (q_t * 0.125).astype(BF16)
    k_all = jnp.dot(
        jnp.concatenate([window, first], axis=0), wk[...], preferred_element_type=F32
    ).astype(BF16)
    v_t = lax.dot_general(wv_t[...], window, NT, preferred_element_type=F32).astype(BF16)
    va_t = lax.dot_general(wv_t[...], first, NT, preferred_element_type=F32).astype(BF16)

    blank = jnp.zeros((64, queries), BF16)
    for i in range(STEP):
        at = STEP * window_rows + i * anchor_rows
        k = jnp.concatenate(
            [k_all[i * window_rows : (i + 1) * window_rows], k_all[at : at + anchor_rows]], axis=0
        )
        for pair in range(pairs):
            at = pair * 128
            across = slice(i * queries, (i + 1) * queries)
            left = jnp.concatenate([q_t[at : at + 64, across], blank], axis=0)
            right = jnp.concatenate([blank, q_t[at + 64 : at + 128, across]], axis=0)
            column = (i * pairs + pair) * 2 * queries
            scores[:, column : column + 2 * queries] = jnp.dot(
                k[:, at : at + 128],
                jnp.concatenate([left, right], axis=1),
                preferred_element_type=F32,
            )

    sub = lax.broadcasted_iota(jnp.int32, (GROUP, queries), 0)
    lane = lax.broadcasted_iota(jnp.int32, (GROUP, queries), 1)
    t = lane // GROUP
    met = (sub - lane + queries) % GROUP

    def slab(u, c):
        return scores[u * GROUP : (u + 1) * GROUP, c * queries : (c + 1) * queries]

    merged = []
    for b in range(WINDOW // GROUP):
        u = met + b * GROUP
        place = jnp.where(u <= t, u, u + WINDOW)
        w = [slab(b * GROUP, c) for c in range(columns)]
        for d in range(GROUP):
            for u in (b * GROUP + d, WINDOW + b * GROUP + d):
                if u != b * GROUP:
                    here = place == u
                    w = [jnp.where(here, slab(u, c), w[c]) for c in range(columns)]
        seen = (place < WINDOW) | (tm > 0)
        merged.append([jnp.where(seen, v, -1e30) for v in w])
    w = [slab(2 * WINDOW, c) for c in range(columns)]
    for u in range(1, ANCHORS):
        here = met == u
        w = [jnp.where(here, slab(2 * WINDOW + u, c), w[c]) for c in range(columns)]
    seen = (met < ANCHORS) & (met < tm * WINDOW + t - (WINDOW - 1))
    merged.append([jnp.where(seen, v, -1e30) for v in w])

    merged = [jnp.concatenate(w, axis=1) for w in merged]
    top = jnp.max(
        jnp.maximum(jnp.maximum(merged[0], merged[1]), merged[2]), axis=0, keepdims=True
    )
    e = [jnp.exp(w - top) for w in merged]
    over = 1.0 / jnp.sum(e[0] + e[1] + e[2], axis=0, keepdims=True)
    probs = [w * over for w in e]
    probs = [jnp.concatenate([w, w], axis=0).astype(BF16) for w in probs]

    for j in range(slabs // 2):
        b = (2 * j % WINDOW) // GROUP if j < WINDOW else 2
        here = mask[j * 16 : (j + 1) * 16, :]
        for c in range(columns):
            piece = probs[b][:, c * queries : (c + 1) * queries] * here
            across = slice(c * queries, (c + 1) * queries)
            if j < WINDOW:
                spread[j * 16 : (j + 1) * 16, across] = piece
            else:
                at = c // (2 * pairs) * anchor_rows + (j - WINDOW) * 16
                spread_first[at : at + 16, across] = piece

    attended = []
    for i in range(STEP):
        parts = []
        for pair in range(pairs):
            at = slice(pair * 128, (pair + 1) * 128)
            column = (i * pairs + pair) * 2 * queries
            across = slice(column, column + 2 * queries)
            o = jnp.dot(
                v_t[at, i * window_rows : (i + 1) * window_rows],
                spread[:, across],
                preferred_element_type=F32,
            )
            o += jnp.dot(va_t[at], spread_first[:, across], preferred_element_type=F32)
            parts += [o[:64, :queries], o[64:, queries:]]
        attended.append(jnp.concatenate(parts, axis=0).astype(BF16))
    attended = jnp.concatenate(attended, axis=1)
    result = lax.dot_general(attended, w_out[...], TN, preferred_element_type=F32)
    results = []
    for i in range(STEP):
        mixed = jnp.concatenate([m_lo[i], m_hi[i]], axis=0)
        total = result[i * queries : (i + 1) * queries] + mixed
        results.append(total.reshape(WINDOW, GROUP, width))
    out[...] = jnp.concatenate(results, axis=1).astype(BF16).reshape(out.shape)


def params():
    return pltpu.CompilerParams(vmem_limit_bytes=VMEM_LIMIT)


def small():
    return pl.CostEstimate(flops=1000, bytes_accessed=1000, transcendentals=0)


def whole(a):
    return pl.BlockSpec(a.shape, lambda f: (0,) * a.ndim)


def row_outputs(count, positions, width):
    groups = positions // GROUP
    spec = pl.BlockSpec((groups, 2 * GROUP, width), lambda f: (0, f, 0))
    shapes = [
        jax.ShapeDtypeStruct((groups, count * GROUP, width), dtype) for dtype in (F32, BF16, BF16)
    ]
    return [spec] * 3, shapes


def embed(first, count, ids, frames, actions, table, conv, gain):
    _, row_count, cols, width = frames.shape
    strip = jax.ShapeDtypeStruct((count, cols, width), BF16)
    strip_spec = pl.BlockSpec((2, cols, width), lambda f: (f, 0, 0))
    block = (2, row_count, cols, width)
    skip = first // 2
    specs, shapes = row_outputs(count, (row_count - 2) * cols, width)
    return pl.pallas_call(
        functools.partial(embed_kernel, first),
        grid=(count // 2,),
        in_specs=[
            pl.BlockSpec((1, 1, 2 * row_count * cols), lambda f: (f + skip, 0, 0)),
            pl.BlockSpec(block, lambda f: (f + skip, 0, 0, 0)),
            whole(actions),
            whole(table),
            whole(conv),
            whole(gain),
        ],
        out_specs=[pl.BlockSpec(block, lambda f: (f, 0, 0, 0)), strip_spec, strip_spec] + specs,
        out_shape=[
            jax.ShapeDtypeStruct((count, row_count, cols, width), BF16),
            strip,
            strip,
        ]
        + shapes,
        compiler_params=params(),
        cost_estimate=small(),
        name="embed",
    )(ids, frames, actions, table, conv, gain)


def edge(first, emb, before, after, conv, gain):
    count, row_count, cols, width = emb.shape
    strip_spec = pl.BlockSpec((2, cols, width), lambda f: (f, 0, 0))
    frame_spec = pl.BlockSpec((2, row_count, cols, width), lambda f: (f, 0, 0, 0))
    specs, shapes = row_outputs(count, 2 * cols, width)
    return pl.pallas_call(
        functools.partial(edge_kernel, first),
        grid=(count // 2,),
        in_specs=[frame_spec, strip_spec, strip_spec, whole(conv), whole(gain)],
        out_specs=specs,
        out_shape=shapes,
        compiler_params=params(),
        cost_estimate=small(),
        name="edge",
    )(emb, before, after, conv, gain)


def attend(tm, blocks, weights, out, shape, positions, row_of):
    count, _, cols, width = shape
    per_row = cols // (STEP * GROUP)
    keys = (2 * WINDOW + ANCHORS) * GROUP
    lanes = STEP * (width // 64) * WINDOW * GROUP

    def block(a, start):
        return pl.BlockSpec((STEP,) + a.shape[1:], lambda g: (g + start // STEP, 0, 0))

    args = [tm, *[a for a, _ in blocks], *weights]
    specs = [pl.BlockSpec(memory_space=pltpu.SMEM)]
    specs += [block(a, start) for a, start in blocks] + [whole(w) for w in weights]
    aliases = {}
    if out is not None:
        aliases = {len(args): 0}
        args.append(out)
        specs.append(pl.BlockSpec(memory_space=pl.ANY))
    return pl.pallas_call(
        attend_kernel,
        grid=(positions // (STEP * GROUP),),
        in_specs=specs,
        out_specs=pl.BlockSpec(
            (count, 1, STEP * GROUP, width),
            lambda g: (0, row_of(g // per_row), g % per_row, 0),
        ),
        out_shape=jax.ShapeDtypeStruct(shape, BF16),
        scratch_shapes=[
            pltpu.VMEM((keys, WINDOW * GROUP), BF16),
            pltpu.VMEM((keys, lanes), F32),
            pltpu.VMEM((2 * WINDOW * GROUP, lanes), BF16),
            pltpu.VMEM((STEP * ANCHORS * GROUP, lanes), BF16),
        ],
        input_output_aliases=aliases,
        compiler_params=params(),
        cost_estimate=small(),
        name="attend",
    )(*args)


def send(x, by):
    count = lax.axis_size("tm")
    return lax.ppermute(x, "tm", [(i, i + by) for i in range(count - by)])


def anchors_of(first, lo, tm):
    count = lax.axis_size("tm")
    anchors = jnp.where(tm == 0, first, lo)
    by = count // 2
    early = None
    while by >= 2:
        pairs = [(i, i + by) for i in range(count - by) if i % (2 * by) < 2]
        got = lax.ppermute(anchors, "tm", pairs)
        early = got if early is None else early
        place = tm % (2 * by)
        anchors = jnp.where((place == by) | (place == by + 1), got, anchors)
        by //= 2
    return anchors, early


def halo(top, bottom):
    strips = lax.axis_size("space")
    up = [(i, i + 1) for i in range(strips - 1)]
    return lax.ppermute(bottom, "space", up), lax.ppermute(top, "space", [(j, i) for i, j in up])


def on_device(
    frames,
    token_ids,
    action_ids,
    token_table,
    action_table,
    conv_weight,
    norm_gain,
    w_query,
    w_key,
    w_value,
    w_out,
):
    shape = frames.shape
    width = shape[3]
    tm = lax.axis_index("tm")
    tm_arg = tm.astype(jnp.int32).reshape(1)
    ids = token_ids.reshape(shape[0] // 2, 1, -1)
    onehot = (action_ids[:, None] == jnp.arange(ACTIONS, dtype=jnp.int32)[None, :]).astype(BF16)
    actions = jnp.dot(onehot, action_table, preferred_element_type=F32)
    conv = conv_weight.reshape(9, width).astype(F32)
    gain = norm_gain.reshape(1, width).astype(F32)
    weights = [w_query.T, w_key, w_value.T, w_out]

    cols = shape[2]
    inner = (shape[1] - 2) * cols // GROUP
    row = cols // GROUP
    shared = (ids, frames, actions, token_table, conv, gain)

    emb, top, bottom, mixed_a, normed_a, rolled_a = embed(0, ANCHORS, *shared)
    mixed_b, normed_b, rolled_b = edge(0, emb, *halo(top, bottom), conv, gain)
    first = jnp.concatenate([rolled_a, rolled_b], axis=0)
    lo = send(first, 1)
    emb, top, bottom, mixed_c, normed_c, rolled_c = embed(ANCHORS, shape[0] - ANCHORS, *shared)
    hi = [send(rolled_c[:row], 1)]
    lo, rest, _ = lax.optimization_barrier((lo, rolled_c, hi[0]))
    hi += [send(rest[r * row : (r + 1) * row], 1) for r in range(1, inner // row)]
    anchors, early = anchors_of(first, lo, tm)
    mixed_d, normed_d, rolled_d = edge(ANCHORS, emb, *halo(top, bottom), conv, gain)

    def blocks(x_lo, x_hi, own_hi, hi, m_lo, m_hi, start, at, hi_at):
        return [
            (x_lo, at),
            (x_hi, at),
            (first, start + at),
            (own_hi, at),
            (lo, start + at),
            (hi, hi_at),
            (anchors, start + at),
            (m_lo, at),
            (m_hi, at),
        ]

    out = None
    for r in range(inner // row):
        out = attend(
            tm_arg,
            blocks(normed_a, normed_c, rolled_c, hi[r], mixed_a, mixed_c, 0, r * row, 0),
            weights,
            out,
            shape,
            cols,
            lambda _, r=r: r + 1,
        )
    to_send, *_ = lax.optimization_barrier((rolled_d, early, *hi[1:]))
    later = [send(to_send[r * row : (r + 1) * row], 1) for r in range(2)]
    for r in range(2):
        out = attend(
            tm_arg,
            blocks(normed_b, normed_d, rolled_d, later[r], mixed_b, mixed_d, inner, r * row, 0),
            weights,
            out,
            shape,
            cols,
            lambda _, r=r: r * (shape[1] - 1),
        )
    return out


def solution(mesh):
    in_specs = (
        P("tm", "space", None, None),
        P(None, "tm", "space", None),
        P("tm"),
        P(),
        P(),
        P(),
        P(),
        P(),
        P(),
        P(),
        P(),
    )
    out_specs = P("tm", "space", None, None)
    return jax.shard_map(
        on_device, mesh=mesh, in_specs=in_specs, out_specs=out_specs, check_vma=False
    )
```

```python
import functools

import jax
import jax.numpy as jnp
from jax import lax
from jax.experimental import pallas as pl
from jax.experimental.pallas import tpu as pltpu
from jax.sharding import PartitionSpec as P

HEADS = 6
ACTIONS = 8
WINDOW = 16
ANCHORS = 4
GROUP = 8
STEP = 4
F32 = jnp.float32
BF16 = jnp.bfloat16
NT = (((1,), (1,)), ((), ()))
TN = (((0,), (0,)), ((), ()))
VMEM_LIMIT = 48 * 1024 * 1024


def shift_cols(y, by):
    cols = y.shape[0]
    rolled = pltpu.roll(y, by % cols, 0)
    at = lax.broadcasted_iota(jnp.int32, y.shape, 0)
    edge = 0 if by == 1 else cols - 1
    return jnp.where(at == edge, 0.0, rolled)


def conv_norm(above, here, below, conv, gain):
    rows = [r.astype(F32) for r in (above, here, below)]
    sums = []
    for j in range(3):
        sums.append(
            rows[0] * conv[j : j + 1]
            + rows[1] * conv[3 + j : 4 + j]
            + rows[2] * conv[6 + j : 7 + j]
        )
    mixed = rows[1] + sums[1] + shift_cols(sums[0], 1) + shift_cols(sums[2], -1)
    scale = lax.rsqrt(jnp.mean(mixed * mixed, axis=-1, keepdims=True) + 1e-06)
    return mixed, mixed * scale * gain


def grouped(first, second):
    width = first.shape[-1]
    first = first.reshape(-1, GROUP, width)
    second = second.reshape(-1, GROUP, width)
    return jnp.concatenate([first, second], axis=1)


def put_rows(first, results, mixed, normed, rolled):
    frame = pl.program_id(0) * 2 + first
    turned = []
    for k in range(2):
        n = results[k][1].reshape(-1, GROUP, results[k][1].shape[-1])
        turned.append(pltpu.roll(n, lax.rem(frame + k, GROUP), 1))
    mixed[...] = grouped(results[0][0], results[1][0])
    normed[...] = grouped(results[0][1], results[1][1]).astype(BF16)
    rolled[...] = jnp.concatenate(turned, axis=1).astype(BF16)


def embed_kernel(
    first, ids, frames, actions, table, conv_ref, gain_ref, emb, top, bottom, mixed, normed, rolled
):
    frame = pl.program_id(0) * 2 + first
    row_count, cols, width = frames.shape[1:]
    vocab = table.shape[0]
    count = 2 * row_count * cols
    row_ids = ids[0].astype(F32)
    codes = jnp.transpose(jnp.broadcast_to(row_ids, (128, count)), (1, 0))
    lane = lax.broadcasted_iota(jnp.int32, (count, 128), 1).astype(F32)
    onehot = [
        jnp.where(codes == lane + 128.0 * k, 1.0, 0.0).astype(BF16) for k in range(vocab // 128)
    ]
    tokens = jnp.dot(jnp.concatenate(onehot, axis=1), table[...], preferred_element_type=F32)
    conv = conv_ref[...]
    gain = gain_ref[...]
    results = []
    for k in range(2):
        action = actions[pl.ds(frame + k, 1), :]
        rows = []
        for r in range(row_count):
            at = (k * row_count + r) * cols
            row = frames[k, r].astype(F32) + tokens[at : at + cols] + action
            row = row.astype(BF16)
            emb[k, r] = row
            rows.append(row)
        top[k] = rows[0]
        bottom[k] = rows[-1]
        done = [
            conv_norm(rows[r - 1], rows[r], rows[r + 1], conv, gain)
            for r in range(1, row_count - 1)
        ]
        results.append([jnp.concatenate(part, axis=0) for part in zip(*done)])
    put_rows(first, results, mixed, normed, rolled)


def edge_kernel(first, emb, before, after, conv_ref, gain_ref, mixed, normed, rolled):
    row_count = emb.shape[1]
    conv = conv_ref[...]
    gain = gain_ref[...]
    results = []
    for k in range(2):
        done = [
            conv_norm(before[k], emb[k, 0], emb[k, 1], conv, gain),
            conv_norm(emb[k, row_count - 2], emb[k, row_count - 1], after[k], conv, gain),
        ]
        results.append([jnp.concatenate(part, axis=0) for part in zip(*done)])
    put_rows(first, results, mixed, normed, rolled)


def attend_kernel(
    tm_ref, x_lo, x_hi, own_lo, own_hi, lo, hi, anchors, m_lo, m_hi, wq_t, wk, wv_t, w_out, *rest
):
    out, mask, scores, spread, spread_first = rest[-5:]
    tm = tm_ref[0]
    width = x_lo.shape[-1]
    queries = WINDOW * GROUP
    pairs = width // 128
    columns = STEP * pairs * 2
    slabs = 2 * WINDOW + ANCHORS
    anchor_rows = ANCHORS * GROUP
    window_rows = 2 * queries

    @pl.when(pl.program_id(0) == 0)
    def _():
        row = lax.broadcasted_iota(jnp.int32, (slabs * GROUP, queries), 0)
        lane = lax.broadcasted_iota(jnp.int32, (slabs * GROUP, queries), 1)
        u = row // GROUP
        t = lane // GROUP
        met = (row - lane + queries) % GROUP
        mine = (u < WINDOW) & (u % GROUP == met) & (u <= t)
        past = (u >= WINDOW) & (u < 2 * WINDOW) & (u % GROUP == met) & (u - WINDOW > t)
        first = (u >= 2 * WINDOW) & (u - 2 * WINDOW == met)
        mask[...] = jnp.where(mine | past | first, 1.0, 0.0).astype(BF16)
        spread_first[...] = jnp.zeros(spread_first.shape, BF16)

    x = jnp.concatenate([ref[i] for i in range(STEP) for ref in (x_lo, x_hi)], axis=0)
    window = [ref[i] for i in range(STEP) for ref in (own_lo, own_hi, lo, hi)]
    window = jnp.concatenate(window, axis=0)
    first = anchors[...].reshape(STEP * anchor_rows, width)
    q_t = lax.dot_general(wq_t[...], x, NT, preferred_element_type=F32).astype(BF16)
    q_t = (q_t * 0.125).astype(BF16)
    k_all = jnp.dot(
        jnp.concatenate([window, first], axis=0), wk[...], preferred_element_type=F32
    ).astype(BF16)
    v_t = lax.dot_general(wv_t[...], window, NT, preferred_element_type=F32).astype(BF16)
    va_t = lax.dot_general(wv_t[...], first, NT, preferred_element_type=F32).astype(BF16)

    blank = jnp.zeros((64, queries), BF16)
    for i in range(STEP):
        at = STEP * window_rows + i * anchor_rows
        k = jnp.concatenate(
            [k_all[i * window_rows : (i + 1) * window_rows], k_all[at : at + anchor_rows]], axis=0
        )
        for pair in range(pairs):
            at = pair * 128
            across = slice(i * queries, (i + 1) * queries)
            left = jnp.concatenate([q_t[at : at + 64, across], blank], axis=0)
            right = jnp.concatenate([blank, q_t[at + 64 : at + 128, across]], axis=0)
            column = (i * pairs + pair) * 2 * queries
            scores[:, column : column + 2 * queries] = jnp.dot(
                k[:, at : at + 128],
                jnp.concatenate([left, right], axis=1),
                preferred_element_type=F32,
            )

    sub = lax.broadcasted_iota(jnp.int32, (GROUP, queries), 0)
    lane = lax.broadcasted_iota(jnp.int32, (GROUP, queries), 1)
    t = lane // GROUP
    met = (sub - lane + queries) % GROUP

    def slab(u, c):
        return scores[u * GROUP : (u + 1) * GROUP, c * queries : (c + 1) * queries]

    merged = []
    for b in range(WINDOW // GROUP):
        u = met + b * GROUP
        place = jnp.where(u <= t, u, u + WINDOW)
        w = [slab(b * GROUP, c) for c in range(columns)]
        for d in range(GROUP):
            for u in (b * GROUP + d, WINDOW + b * GROUP + d):
                if u != b * GROUP:
                    here = place == u
                    w = [jnp.where(here, slab(u, c), w[c]) for c in range(columns)]
        seen = (place < WINDOW) | (tm > 0)
        merged.append([jnp.where(seen, v, -1e30) for v in w])
    w = [slab(2 * WINDOW, c) for c in range(columns)]
    for u in range(1, ANCHORS):
        here = met == u
        w = [jnp.where(here, slab(2 * WINDOW + u, c), w[c]) for c in range(columns)]
    seen = (met < ANCHORS) & (met < tm * WINDOW + t - (WINDOW - 1))
    merged.append([jnp.where(seen, v, -1e30) for v in w])

    merged = [jnp.concatenate(w, axis=1) for w in merged]
    top = jnp.max(
        jnp.maximum(jnp.maximum(merged[0], merged[1]), merged[2]), axis=0, keepdims=True
    )
    e = [jnp.exp(w - top) for w in merged]
    over = 1.0 / jnp.sum(e[0] + e[1] + e[2], axis=0, keepdims=True)
    probs = [w * over for w in e]
    probs = [jnp.concatenate([w, w], axis=0).astype(BF16) for w in probs]

    for j in range(slabs // 2):
        b = (2 * j % WINDOW) // GROUP if j < WINDOW else 2
        here = mask[j * 16 : (j + 1) * 16, :]
        for c in range(columns):
            piece = probs[b][:, c * queries : (c + 1) * queries] * here
            across = slice(c * queries, (c + 1) * queries)
            if j < WINDOW:
                spread[j * 16 : (j + 1) * 16, across] = piece
            else:
                at = c // (2 * pairs) * anchor_rows + (j - WINDOW) * 16
                spread_first[at : at + 16, across] = piece

    attended = []
    for i in range(STEP):
        parts = []
        for pair in range(pairs):
            at = slice(pair * 128, (pair + 1) * 128)
            column = (i * pairs + pair) * 2 * queries
            across = slice(column, column + 2 * queries)
            o = jnp.dot(
                v_t[at, i * window_rows : (i + 1) * window_rows],
                spread[:, across],
                preferred_element_type=F32,
            )
            o += jnp.dot(va_t[at], spread_first[:, across], preferred_element_type=F32)
            parts += [o[:64, :queries], o[64:, queries:]]
        attended.append(jnp.concatenate(parts, axis=0).astype(BF16))
    attended = jnp.concatenate(attended, axis=1)
    result = lax.dot_general(attended, w_out[...], TN, preferred_element_type=F32)
    results = []
    for i in range(STEP):
        mixed = jnp.concatenate([m_lo[i], m_hi[i]], axis=0)
        total = result[i * queries : (i + 1) * queries] + mixed
        results.append(total.reshape(WINDOW, GROUP, width))
    out[...] = jnp.concatenate(results, axis=1).astype(BF16).reshape(out.shape)


def params():
    return pltpu.CompilerParams(vmem_limit_bytes=VMEM_LIMIT)


def small():
    return pl.CostEstimate(flops=1000, bytes_accessed=1000, transcendentals=0)


def whole(a):
    return pl.BlockSpec(a.shape, lambda f: (0,) * a.ndim)


def row_outputs(count, positions, width):
    groups = positions // GROUP
    spec = pl.BlockSpec((groups, 2 * GROUP, width), lambda f: (0, f, 0))
    shapes = [
        jax.ShapeDtypeStruct((groups, count * GROUP, width), dtype) for dtype in (F32, BF16, BF16)
    ]
    return [spec] * 3, shapes


def embed(first, count, ids, frames, actions, table, conv, gain):
    _, row_count, cols, width = frames.shape
    strip = jax.ShapeDtypeStruct((count, cols, width), BF16)
    strip_spec = pl.BlockSpec((2, cols, width), lambda f: (f, 0, 0))
    block = (2, row_count, cols, width)
    skip = first // 2
    specs, shapes = row_outputs(count, (row_count - 2) * cols, width)
    return pl.pallas_call(
        functools.partial(embed_kernel, first),
        grid=(count // 2,),
        in_specs=[
            pl.BlockSpec((1, 1, 2 * row_count * cols), lambda f: (f + skip, 0, 0)),
            pl.BlockSpec(block, lambda f: (f + skip, 0, 0, 0)),
            whole(actions),
            whole(table),
            whole(conv),
            whole(gain),
        ],
        out_specs=[pl.BlockSpec(block, lambda f: (f, 0, 0, 0)), strip_spec, strip_spec] + specs,
        out_shape=[
            jax.ShapeDtypeStruct((count, row_count, cols, width), BF16),
            strip,
            strip,
        ]
        + shapes,
        compiler_params=params(),
        cost_estimate=small(),
        name="embed",
    )(ids, frames, actions, table, conv, gain)


def edge(first, emb, before, after, conv, gain):
    count, row_count, cols, width = emb.shape
    strip_spec = pl.BlockSpec((2, cols, width), lambda f: (f, 0, 0))
    frame_spec = pl.BlockSpec((2, row_count, cols, width), lambda f: (f, 0, 0, 0))
    specs, shapes = row_outputs(count, 2 * cols, width)
    return pl.pallas_call(
        functools.partial(edge_kernel, first),
        grid=(count // 2,),
        in_specs=[frame_spec, strip_spec, strip_spec, whole(conv), whole(gain)],
        out_specs=specs,
        out_shape=shapes,
        compiler_params=params(),
        cost_estimate=small(),
        name="edge",
    )(emb, before, after, conv, gain)


def attend(tm, blocks, weights, out, shape, positions, row_of):
    count, _, cols, width = shape
    per_row = cols // (STEP * GROUP)
    keys = (2 * WINDOW + ANCHORS) * GROUP
    lanes = STEP * (width // 64) * WINDOW * GROUP

    def block(a, start):
        return pl.BlockSpec((STEP,) + a.shape[1:], lambda g: (g + start // STEP, 0, 0))

    args = [tm, *[a for a, _ in blocks], *weights]
    specs = [pl.BlockSpec(memory_space=pltpu.SMEM)]
    specs += [block(a, start) for a, start in blocks] + [whole(w) for w in weights]
    aliases = {}
    if out is not None:
        aliases = {len(args): 0}
        args.append(out)
        specs.append(pl.BlockSpec(memory_space=pl.ANY))
    return pl.pallas_call(
        attend_kernel,
        grid=(positions // (STEP * GROUP),),
        in_specs=specs,
        out_specs=pl.BlockSpec(
            (count, 1, STEP * GROUP, width),
            lambda g: (0, row_of(g // per_row), g % per_row, 0),
        ),
        out_shape=jax.ShapeDtypeStruct(shape, BF16),
        scratch_shapes=[
            pltpu.VMEM((keys, WINDOW * GROUP), BF16),
            pltpu.VMEM((keys, lanes), F32),
            pltpu.VMEM((2 * WINDOW * GROUP, lanes), BF16),
            pltpu.VMEM((STEP * ANCHORS * GROUP, lanes), BF16),
        ],
        input_output_aliases=aliases,
        compiler_params=params(),
        cost_estimate=small(),
        name="attend",
    )(*args)


def send(x, by):
    count = lax.axis_size("tm")
    return lax.ppermute(x, "tm", [(i, i + by) for i in range(count - by)])


def anchors_of(first, lo, tm):
    count = lax.axis_size("tm")
    anchors = jnp.where(tm == 0, first, lo)
    by = count // 2
    while by >= 2:
        pairs = [(i, i + by) for i in range(count - by) if i % (2 * by) < 2]
        got = lax.ppermute(anchors, "tm", pairs)
        place = tm % (2 * by)
        anchors = jnp.where((place == by) | (place == by + 1), got, anchors)
        by //= 2
    return anchors


def halo(top, bottom):
    strips = lax.axis_size("space")
    up = [(i, i + 1) for i in range(strips - 1)]
    return lax.ppermute(bottom, "space", up), lax.ppermute(top, "space", [(j, i) for i, j in up])


def on_device(
    frames,
    token_ids,
    action_ids,
    token_table,
    action_table,
    conv_weight,
    norm_gain,
    w_query,
    w_key,
    w_value,
    w_out,
):
    shape = frames.shape
    width = shape[3]
    tm = lax.axis_index("tm")
    tm_arg = tm.astype(jnp.int32).reshape(1)
    ids = token_ids.reshape(shape[0] // 2, 1, -1)
    onehot = (action_ids[:, None] == jnp.arange(ACTIONS, dtype=jnp.int32)[None, :]).astype(BF16)
    actions = jnp.dot(onehot, action_table, preferred_element_type=F32)
    conv = conv_weight.reshape(9, width).astype(F32)
    gain = norm_gain.reshape(1, width).astype(F32)
    weights = [w_query.T, w_key, w_value.T, w_out]

    cols = shape[2]
    inner = (shape[1] - 2) * cols // GROUP
    row = cols // GROUP
    shared = (ids, frames, actions, token_table, conv, gain)

    emb, top, bottom, mixed_a, normed_a, rolled_a = embed(0, ANCHORS, *shared)
    mixed_b, normed_b, rolled_b = edge(0, emb, *halo(top, bottom), conv, gain)
    first = jnp.concatenate([rolled_a, rolled_b], axis=0)
    lo = send(first, 1)
    emb, top, bottom, mixed_c, normed_c, rolled_c = embed(ANCHORS, shape[0] - ANCHORS, *shared)
    lo, _ = lax.optimization_barrier((lo, rolled_c))
    anchors = anchors_of(first, lo, tm)
    hi = [send(rolled_c[r * row : (r + 1) * row], 1) for r in range(inner // row)]
    top, bottom, _ = lax.optimization_barrier((top, bottom, hi[0]))
    mixed_d, normed_d, rolled_d = edge(ANCHORS, emb, *halo(top, bottom), conv, gain)

    def blocks(x_lo, x_hi, own_hi, hi, m_lo, m_hi, start, at, hi_at):
        return [
            (x_lo, at),
            (x_hi, at),
            (first, start + at),
            (own_hi, at),
            (lo, start + at),
            (hi, hi_at),
            (anchors, start + at),
            (m_lo, at),
            (m_hi, at),
        ]

    out = None
    for r in range(inner // row):
        out = attend(
            tm_arg,
            blocks(normed_a, normed_c, rolled_c, hi[r], mixed_a, mixed_c, 0, r * row, 0),
            weights,
            out,
            shape,
            cols,
            lambda _, r=r: r + 1,
        )
    to_send, _ = lax.optimization_barrier((rolled_d, hi[0]))
    later = [send(to_send[r * row : (r + 1) * row], 1) for r in range(2)]
    for r in range(2):
        out = attend(
            tm_arg,
            blocks(normed_b, normed_d, rolled_d, later[r], mixed_b, mixed_d, inner, r * row, 0),
            weights,
            out,
            shape,
            cols,
            lambda _, r=r: r * (shape[1] - 1),
        )
    return out


def solution(mesh):
    in_specs = (
        P("tm", "space", None, None),
        P(None, "tm", "space", None),
        P("tm"),
        P(),
        P(),
        P(),
        P(),
        P(),
        P(),
        P(),
        P(),
    )
    out_specs = P("tm", "space", None, None)
    return jax.shard_map(
        on_device, mesh=mesh, in_specs=in_specs, out_specs=out_specs, check_vma=False
    )
```
